256 devices in a mesh: flow: 4 (over x), tile: 64 (over z, y, core).
Axes of the slice: x: 4, y: 4, z: 8, core: 2. Of those that a mesh axis runs over, the one named last changes fastest.
Arguments:
- right_side: float32 [4, 64, 4, 64, 128], P('flow', 'tile'), may hold values from -6 to 6
- fine_diag: bfloat16 [4, 64, 64, 64, 128], P('flow', 'tile'), may hold values from -0.41 to 3.41
- fine_inverse: bfloat16 [4, 64, 64, 64, 128], P('flow', 'tile'), may hold values from -0.11 to 0.71
- fine_faces: bfloat16 [4, 64, 3, 64, 64, 128], P('flow', 'tile'), may hold values from -0.359375 to 0.359375
- fine_links: int32 [4, 64, 3, 128], P('flow', 'tile'), may hold values from 0 to 127, each once within a row
- fine_order: int32 [4, 64, 128], P('flow', 'tile'), may hold values from 0 to 127, each once within a row
- fine_picks: int32 [4, 64, 2, 64], P('flow', 'tile'), may hold values from 0 to 63
- fine_weights: bfloat16 [4, 64, 2, 64, 64, 64], P('flow', 'tile'), may hold values from -0.59765625 to 0.59765625
- middle_diag: bfloat16 [4, 64, 64, 64, 64], P('flow', 'tile'), may hold values from -0.41 to 3.41
- middle_inverse: bfloat16 [4, 64, 64, 64, 64], P('flow', 'tile'), may hold values from -0.11 to 0.71
- middle_faces: bfloat16 [4, 64, 3, 64, 64, 64], P('flow', 'tile'), may hold values from -0.359375 to 0.359375
- middle_links: int32 [4, 64, 3, 64], P('flow', 'tile'), may hold values from 0 to 63, each once within a row
- middle_order: int32 [4, 64, 64], P('flow', 'tile'), may hold values from 0 to 63, each once within a row
- middle_picks: int32 [4, 64, 2, 32], P('flow', 'tile'), may hold values from 0 to 31
- middle_weights: bfloat16 [4, 64, 2, 64, 64, 32], P('flow', 'tile'), may hold values from -0.59765625 to 0.59765625
- coarse_inverse: bfloat16 [4, 64, 64, 64, 32], P('flow', 'tile'), may hold values from -0.11 to 0.71
- coarse_faces: bfloat16 [4, 64, 3, 64, 64, 32], P('flow', 'tile'), may hold values from -0.359375 to 0.359375
- coarse_links: int32 [4, 64, 3, 32], P('flow', 'tile'), may hold values from 0 to 31, each once within a row
Outputs:
- solution: float32 [4, 64, 4, 64, 128], P('flow', 'tile')
The draws below stay inside these ranges and needn't reach their ends.
All inputs are finite; a program needn't handle non-finite values.
Results may differ from the reference program's by a relative error of at most 0.0003.
Values may be sent and summed in bfloat16 or wider, within the bound.
No kernel may reach another device: no remote copies, remote signals or barrier semaphores. Data moves between devices by JAX's collectives and lax.ppermute only.
A program may use at most 128 MiB of HBM per device.

```python
import jax
import jax.numpy as jnp
from jax import lax

BLOCK = 64
TRACERS = 4
FACES = 3
RLINKS = 2
SWEEPS = 3
FINE_BLOCKS = 128
MID_BLOCKS = 64
COARSE_BLOCKS = 32
N_FLOW = 4
N_TILE = 64


def diagonal_block(key, blocks, centre_low, centre_high, spread):
    first_key, second_key = jax.random.split(key)
    shape = (N_FLOW, N_TILE, BLOCK, BLOCK, blocks)
    centre = jax.random.uniform(first_key, shape, jnp.float32, centre_low, centre_high)
    noise = jnp.clip(jax.random.normal(second_key, shape, jnp.float32), -4.0, 4.0) * spread
    identity = jnp.eye(BLOCK, dtype=jnp.float32)[:, :, None]
    return identity * centre + noise


def draw_fine_diag(key, part):
    key = jax.random.fold_in(key, 11)
    return diagonal_block(key, FINE_BLOCKS, 1.5, 3.0, 0.1).astype(jnp.bfloat16)


def draw_middle_diag(key, part):
    key = jax.random.fold_in(key, 12)
    return diagonal_block(key, MID_BLOCKS, 1.5, 3.0, 0.1).astype(jnp.bfloat16)


def draw_fine_inverse(key, part):
    key = jax.random.fold_in(key, 21)
    return diagonal_block(key, FINE_BLOCKS, 0.3, 0.6, 0.025).astype(jnp.bfloat16)


def draw_middle_inverse(key, part):
    key = jax.random.fold_in(key, 22)
    return diagonal_block(key, MID_BLOCKS, 0.3, 0.6, 0.025).astype(jnp.bfloat16)


def draw_coarse_inverse(key, part):
    key = jax.random.fold_in(key, 23)
    return diagonal_block(key, COARSE_BLOCKS, 0.3, 0.6, 0.025).astype(jnp.bfloat16)


def plant(values, own_key, smallest, high):
    longest = values.shape.index(max(values.shape))
    spots = []
    for shift in (0, 1):
        where = [jax.random.randint(jax.random.fold_in(own_key, axis), (), 0, length) for axis, length in enumerate(values.shape)]
        where[longest] = (where[longest] + shift) % values.shape[longest]
        spots.append(tuple(where))
    return values.at[spots[0]].set(smallest).at[spots[1]].set(high)


def steps_of(rng, extent, pieces, low, largest):
    level, own = 1.0, jax.random.fold_in(rng, 6)
    for dim, blocks in pieces:
        draws = jnp.exp(jax.random.uniform(jax.random.fold_in(own, dim), (blocks,), jnp.float32, low / len(pieces), largest / len(pieces)))
        level = level * jnp.repeat(draws, extent[dim] // blocks).reshape([-1 if axis == dim else 1 for axis in range(len(extent))])
    return level


def gaussian(own_key, shape, deviation, reach, cuts=(), held_as=jnp.bfloat16):
    drawn = jax.random.normal(own_key, shape, jnp.float32) * deviation
    if len(cuts) > 0:
        drawn = steps_of(own_key, shape, cuts, -0.22, 0.18) * drawn
    return jnp.clip(drawn, min=-reach, max=reach).astype(held_as)


def setup_inputs(seed: int = 0) -> dict:
    keys = jax.random.split(jax.random.key(seed), 19)
    return {
        "right_side": gaussian(keys[0], (N_FLOW, N_TILE, TRACERS, BLOCK, FINE_BLOCKS), 1.0, 6.0, ((0, 4), (1, 64)), jnp.float32),
        "fine_diag": draw_fine_diag(jax.random.fold_in(keys[18], 71), 0),
        "fine_inverse": draw_fine_inverse(jax.random.fold_in(keys[18], 71), 0),
        "fine_faces": gaussian(keys[3], (N_FLOW, N_TILE, FACES, BLOCK, BLOCK, FINE_BLOCKS), 0.06, 0.359375, ((0, 4), (1, 64))),
        "fine_links": jax.vmap(lambda own: jax.random.permutation(own, FINE_BLOCKS))(jax.random.split(keys[4], N_FLOW * N_TILE * FACES)).reshape((N_FLOW, N_TILE, FACES, FINE_BLOCKS)).astype(jnp.int32),
        "fine_order": jax.vmap(lambda own: jax.random.permutation(own, FINE_BLOCKS))(jax.random.split(keys[5], N_FLOW * N_TILE)).reshape((N_FLOW, N_TILE, FINE_BLOCKS)).astype(jnp.int32),
        "fine_picks": plant(jax.random.randint(keys[6], (N_FLOW, N_TILE, RLINKS, MID_BLOCKS), 0, FINE_BLOCKS - MID_BLOCKS), jax.random.fold_in(keys[6], 1), 0, (FINE_BLOCKS - MID_BLOCKS) - 1).astype(jnp.int32),
        "fine_weights": gaussian(keys[7], (N_FLOW, N_TILE, RLINKS, BLOCK, BLOCK, MID_BLOCKS), 0.1, 0.59765625, ((0, 4), (1, 64))),
        "middle_diag": draw_middle_diag(jax.random.fold_in(keys[18], 71), 0),
        "middle_inverse": draw_middle_inverse(jax.random.fold_in(keys[18], 71), 0),
        "middle_faces": gaussian(keys[10], (N_FLOW, N_TILE, FACES, BLOCK, BLOCK, MID_BLOCKS), 0.06, 0.359375, ((0, 4), (1, 64))),
        "middle_links": jax.vmap(lambda own: jax.random.permutation(own, MID_BLOCKS))(jax.random.split(keys[11], N_FLOW * N_TILE * FACES)).reshape((N_FLOW, N_TILE, FACES, MID_BLOCKS)).astype(jnp.int32),
        "middle_order": jax.vmap(lambda own: jax.random.permutation(own, MID_BLOCKS))(jax.random.split(keys[12], N_FLOW * N_TILE)).reshape((N_FLOW, N_TILE, MID_BLOCKS)).astype(jnp.int32),
        "middle_picks": plant(jax.random.randint(keys[13], (N_FLOW, N_TILE, RLINKS, COARSE_BLOCKS), 0, MID_BLOCKS - COARSE_BLOCKS), jax.random.fold_in(keys[13], 1), 0, (MID_BLOCKS - COARSE_BLOCKS) - 1).astype(jnp.int32),
        "middle_weights": gaussian(keys[14], (N_FLOW, N_TILE, RLINKS, BLOCK, BLOCK, COARSE_BLOCKS), 0.1, 0.59765625, ((0, 4), (1, 64))),
        "coarse_inverse": draw_coarse_inverse(jax.random.fold_in(keys[18], 71), 0),
        "coarse_faces": gaussian(keys[16], (N_FLOW, N_TILE, FACES, BLOCK, BLOCK, COARSE_BLOCKS), 0.06, 0.359375, ((0, 4), (1, 64))),
        "coarse_links": jax.vmap(lambda own: jax.random.permutation(own, COARSE_BLOCKS))(jax.random.split(keys[17], N_FLOW * N_TILE * FACES)).reshape((N_FLOW, N_TILE, FACES, COARSE_BLOCKS)).astype(jnp.int32),
    }


def block_product(matrix, vector):
    return jnp.einsum("ije,sje->sie", matrix.astype(jnp.float32), vector, precision=lax.Precision.HIGHEST)


def both_maps(function):
    return jax.vmap(jax.vmap(function))


def local_operator(vector, upstream, beside, diagonal, faces, links):
    result = block_product(diagonal, vector)
    result = result - block_product(faces[0], jnp.take(vector, links[0], axis=2))
    result = result - block_product(faces[1], jnp.take(upstream, links[1], axis=2))
    result = result - block_product(faces[2], jnp.take(beside, links[2], axis=2))
    return result


def operate(field, diagonal, faces, links):
    upstream = jnp.concatenate([jnp.zeros_like(field[:1]), field[:-1]], axis=0)
    beside = jnp.roll(field, 1, axis=1)
    return both_maps(local_operator)(field, upstream, beside, diagonal, faces, links)


def selector(order, coarse_blocks):
    total_blocks = order.shape[0]
    return (order[:coarse_blocks, None] == jnp.arange(total_blocks, dtype=jnp.int32)[None, :]).astype(jnp.float32)


def local_smooth(residual, inverse, order, picks):
    fine_mask = 1.0 - jnp.sum(selector(order, picks.shape[1]), axis=0)
    return fine_mask * block_product(inverse, residual)


def local_restrict(residual, order, picks, weights):
    coarse_blocks = picks.shape[1]
    coarse_ids = order[:coarse_blocks]
    fine_ids = order[coarse_blocks:]
    result = jnp.take(residual, coarse_ids, axis=2)
    for link_slot in range(picks.shape[0]):
        chosen = jnp.take(residual, jnp.take(fine_ids, picks[link_slot]), axis=2)
        result = result + block_product(weights[link_slot], chosen)
    return result


def local_inject(field, coarse, order):
    chooser = selector(order, coarse.shape[2])
    return field + jnp.einsum("sbc,ce->sbe", coarse, chooser, precision=lax.Precision.HIGHEST)


def level_cycle(right_side, diagonal, inverse, faces, links, order, picks, weights, coarse_solve):
    smooth = both_maps(local_smooth)
    field = smooth(right_side, inverse, order, picks)
    residual = right_side - operate(field, diagonal, faces, links)
    restricted = both_maps(local_restrict)(residual, order, picks, weights)
    correction = coarse_solve(restricted)
    field = both_maps(local_inject)(field, correction, order)
    field = field + smooth(right_side - operate(field, diagonal, faces, links), inverse, order, picks)
    return field


def local_known(right_side, previous, beside, faces, links):
    result = right_side + block_product(faces[0], jnp.take(previous, links[0], axis=2))
    return result + block_product(faces[2], jnp.take(beside, links[2], axis=2))


def front_step(known_part, upstream, inverse, face, link):
    return block_product(inverse, known_part + block_product(face, jnp.take(upstream, link, axis=2)))


def coarse_sweeps(right_side, inverse, faces, links):
    previous = jnp.zeros_like(right_side)
    for sweep_step in range(SWEEPS):
        beside = jnp.roll(previous, 1, axis=1)
        known_part = both_maps(local_known)(right_side, previous, beside, faces, links)
        upstream = jnp.zeros_like(right_side[0])
        layers = []
        for group_index in range(N_FLOW):
            upstream = jax.vmap(front_step)(known_part[group_index], upstream, inverse[group_index], faces[group_index][:, 1], links[group_index][:, 1])
            layers.append(upstream)
        previous = jnp.stack(layers)
    return previous


def reference(right_side, fine_diag, fine_inverse, fine_faces, fine_links, fine_order, fine_picks, fine_weights, middle_diag, middle_inverse, middle_faces, middle_links, middle_order, middle_picks, middle_weights, coarse_inverse, coarse_faces, coarse_links):
    def third_level(restricted):
        return coarse_sweeps(restricted, coarse_inverse, coarse_faces, coarse_links)

    def second_level(restricted):
        return level_cycle(restricted, middle_diag, middle_inverse, middle_faces, middle_links, middle_order, middle_picks, middle_weights, third_level)

    return level_cycle(right_side, fine_diag, fine_inverse, fine_faces, fine_links, fine_order, fine_picks, fine_weights, second_level)
```

```python
import functools

import jax
import jax.numpy as jnp
from jax import lax
from jax.experimental import pallas as pl
from jax.experimental.pallas import tpu as pltpu
from jax.sharding import PartitionSpec as P

SWEEPS = 3
S = 4
B = 64
LANES = 128


F_LINK, F_PICK, F_COARSE = 0, 3, 5
M_LINK, M_PICK, M_COARSE, M_FINE = 6, 9, 11, 12
C_LINK, M_POS, TABLE = 13, 16, 24


def lane_index():
    return lax.broadcasted_iota(jnp.int32, (1, LANES), 1)


def take_lanes(x, index):
    rows = x.reshape(-1, LANES)
    index = jnp.broadcast_to(index, rows.shape)
    return jnp.take_along_axis(rows, index, axis=1, mode="promise_in_bounds").reshape(x.shape)


def expand(packed, index, out, scale=None):
    rows = packed.shape[1]
    r = B // rows
    for h in range(r):
        values = take_lanes(packed, index + h * (LANES // r))
        if scale is not None:
            values = values * scale
        out[:, h * rows : (h + 1) * rows, :] = values


def pack(wide, r):
    rows = B // r
    group = lane_index() // (LANES // r)
    result = wide[:, :rows, :]
    for h in range(1, r):
        result = jnp.where(group == h, wide[:, h * rows : (h + 1) * rows, :], result)
    return result


def fold(parts):
    row = lax.broadcasted_iota(jnp.int32, (8, LANES), 0)
    high = row >= 4
    mid = (row & 2) > 0
    low = (row & 1) > 0
    level = []
    for i in range(4):
        a, b = parts[i], parts[i + 4]
        level.append(jnp.where(high, b, a) + pltpu.roll(jnp.where(high, a, b), 4, 0))
    pairs = []
    for i in range(2):
        a, b = level[i], level[i + 2]
        pairs.append(jnp.where(mid, b + pltpu.roll(b, 2, 0), a + pltpu.roll(a, 6, 0)))
    a, b = pairs
    return jnp.where(low, b + pltpu.roll(b, 1, 0), a + pltpu.roll(a, 7, 0))


def products(blocks, fields, rows, emit):
    def body(step, carry):
        base = pl.multiple_of(step * 8, 8)
        parts = [[None] * 8 for _ in range(S)]
        for block, field in zip(blocks, fields):
            for i in range(8):
                matrix = block[base + i].astype(jnp.float32)
                for s in range(S):
                    part = jnp.sum((matrix * field[s]).reshape(8, 8, LANES), axis=0)
                    parts[s][i] = part if parts[s][i] is None else parts[s][i] + part
        for s in range(S):
            emit(s, pl.ds(base, 8), fold(parts[s]))
        return carry

    lax.fori_loop(0, rows // 8, body, 0)


def positions(order, n):
    padded = order if n == LANES else jnp.where(lane_index() < n, order, -1)
    hit = padded == lax.broadcasted_iota(jnp.int32, (LANES, LANES), 0)
    place = lax.broadcasted_iota(jnp.int32, (8, LANES), 1).astype(jnp.float32)
    return lax.dot_general(
        place.astype(jnp.bfloat16),
        hit.astype(jnp.float32).astype(jnp.bfloat16),
        (((1,), (1,)), ((), ())),
        preferred_element_type=jnp.float32,
    )


def start_kernel(b, inverse, order, f0, sent):
    place = positions(order[...], LANES)
    mask = (place[0:1] >= 63.5).astype(jnp.float32)

    def emit(s, rows, tile):
        f0[s, rows, :] = tile * mask

    products([inverse], [b], B, emit)
    lane = lane_index()
    index = take_lanes(jnp.broadcast_to(order[...], (8, LANES)), 64 + lane % 64)[0:1]
    wide = take_lanes(f0[...], index)
    sent[0:128, :] = pack(wide, 2).reshape(128, LANES)
    sent[128:136, :] = place


def prepare_kernel(
    f_links, f_order, f_picks, m_links, m_order, m_picks, c_links,
    m_diag, m_inverse, m_faces, f_weights, c_inverse, c_faces, m_weights,
    table, middle, coarse,
):
    lane = lane_index()

    def spread(row, n):
        return jnp.concatenate([row] * (LANES // n), axis=1)

    def pick(source, index):
        source = jnp.broadcast_to(source, (8, LANES))
        return take_lanes(source, jnp.broadcast_to(index, (8, LANES)))[0:1]

    for k in range(3):
        table[F_LINK + k : F_LINK + k + 1, :] = f_links[k : k + 1, :]
        table[M_LINK + k : M_LINK + k + 1, :] = spread(m_links[k : k + 1, :], 64)
        table[C_LINK + k : C_LINK + k + 1, :] = spread(c_links[k : k + 1, :], 32)
    order = f_order[...]
    wide_order = spread(m_order[...], 64)
    for k in range(2):
        table[F_PICK + k : F_PICK + k + 1, :] = pick(order, 64 + spread(f_picks[k : k + 1, :], 64))
        table[M_PICK + k : M_PICK + k + 1, :] = pick(wide_order, 32 + spread(m_picks[k : k + 1, :], 32))
    table[F_COARSE : F_COARSE + 1, :] = pick(order, lane % 64)
    table[M_COARSE : M_COARSE + 1, :] = pick(wide_order, lane % 32)
    table[M_FINE : M_FINE + 1, :] = pick(wide_order, 32 + lane % 32)
    place = positions(wide_order, 64)
    place = pick(place.astype(jnp.int32), lane % 64)
    table[M_POS:TABLE, :] = jnp.broadcast_to(place, (TABLE - M_POS, LANES))

    def halves(i, carry):
        for slot, source in enumerate(
            [m_diag, m_inverse, m_faces.at[0], m_faces.at[1], m_faces.at[2], f_weights.at[0], f_weights.at[1]]
        ):
            middle[slot, i] = jnp.concatenate([source[i], source[32 + i]], axis=1)
        return carry

    def quarters(i, carry):
        for slot, source in enumerate(
            [c_inverse, c_faces.at[0], c_faces.at[1], c_faces.at[2], m_weights.at[0], m_weights.at[1]]
        ):
            coarse[slot, i] = jnp.concatenate([source[16 * q + i] for q in range(4)], axis=1)
        return carry

    lax.fori_loop(0, 32, halves, 0)
    lax.fori_loop(0, 16, quarters, 0)


M_DIAG, M_INVERSE, M_FACE, F_WEIGHT = 0, 1, 2, 5
C_INVERSE, C_FACE, M_WEIGHT = 0, 1, 4


def row(table, k):
    return table[k : k + 1, :]


def fine_local_kernel(b, f0, diag, faces, links, out, own, linked):
    own[...] = -f0[...]
    linked[...] = take_lanes(f0[...], row(links, 0))

    def emit(s, rows, tile):
        out[s, rows, :] = b[s, rows, :] + tile

    products([diag, faces.at[0]], [own, linked], B, emit)


def chosen(place, index, low, high):
    spot = take_lanes(jnp.broadcast_to(place, (8, LANES)), jnp.broadcast_to(index, (8, LANES)))[0:1]
    inside = (spot >= low) & (spot < high)
    return jnp.clip(spot - low, 0, high - low - 1), inside.astype(jnp.float32)


def fine_down_kernel(
    known, up, beside, faces, table, middle, flow,
    r0, right, f0, sent, v1, v2, wide,
):
    gate = (flow[0] > 0).astype(jnp.float32)
    for v, got, k, scale in ((v1, up, 1, gate), (v2, beside, 2, None)):
        index, inside = chosen(got[128:136, :].astype(jnp.int32)[0:1], row(table, F_LINK + k), 64, 128)
        expand(got[0:128, :].reshape(S, 32, LANES), index, v, inside if scale is None else inside * scale)

    def emit_residual(s, rows, tile):
        r0[s, rows, :] = known[s, rows, :] + tile

    products([faces.at[1], faces.at[2]], [v1, v2], B, emit_residual)
    residual = r0[...]
    v1[...] = take_lanes(residual, row(table, F_PICK))
    v2[...] = take_lanes(residual, row(table, F_PICK + 1))
    wide[...] = take_lanes(residual, row(table, F_COARSE))
    right[...] = pack(wide[...], 2)

    def emit_right(s, rows, tile):
        right[s, rows, :] += tile

    products([middle.at[F_WEIGHT], middle.at[F_WEIGHT + 1]], [v1, v2], 32, emit_right)
    expand(right[...], lane_index() % 64, wide)
    mask = (row(table, M_POS) >= 32).astype(jnp.float32)

    def emit_field(s, rows, tile):
        f0[s, rows, :] = tile * mask

    products([middle.at[M_INVERSE]], [wide], 32, emit_field)
    expand(f0[...], row(table, M_FINE), wide)
    sent[0:64, :] = pack(wide[...], 4).reshape(64, LANES)
    sent[64:72, :] = table[M_POS:TABLE, :].astype(jnp.float32)


def middle_local_kernel(b, f0, middle, table, out, own, linked):
    expand(-f0[...], lane_index() % 64, own)
    expand(f0[...], row(table, M_LINK), linked)

    def emit(s, rows, tile):
        out[s, rows, :] = b[s, rows, :] + tile

    products([middle.at[M_DIAG], middle.at[M_FACE]], [own, linked], 32, emit)


def middle_down_kernel(
    known, up, beside, middle, coarse, table, flow,
    r0, right, first, v1, v2, wide,
):
    gate = (flow[0] > 0).astype(jnp.float32)
    for v, got, k, scale in ((v1, up, 1, gate), (v2, beside, 2, None)):
        index, inside = chosen(got[64:72, :].astype(jnp.int32)[0:1], row(table, M_LINK + k), 32, 64)
        expand(got[0:64, :].reshape(S, 16, LANES), index, v, inside if scale is None else inside * scale)

    def emit_residual(s, rows, tile):
        r0[s, rows, :] = known[s, rows, :] + tile

    products([middle.at[M_FACE + 1], middle.at[M_FACE + 2]], [v1, v2], 32, emit_residual)
    residual = r0[...]
    expand(residual, row(table, M_PICK), v1)
    expand(residual, row(table, M_PICK + 1), v2)
    expand(residual, row(table, M_COARSE), wide)
    right[...] = pack(wide[...], 4)

    def emit_right(s, rows, tile):
        right[s, rows, :] += tile

    products([coarse.at[M_WEIGHT], coarse.at[M_WEIGHT + 1]], [v1, v2], 16, emit_right)
    expand(right[...], lane_index() % 32, wide)
    start = (flow[0] == 0).astype(jnp.float32)

    def emit_first(s, rows, tile):
        first[s, rows, :] = tile * start

    products([coarse.at[C_INVERSE]], [wide], 16, emit_first)


def coarse_local_kernel(right, own, coarse, table, out, wide):
    expand(own[...], row(table, C_LINK), wide)

    def emit(s, rows, tile):
        out[s, rows, :] = right[s, rows, :] + tile

    products([coarse.at[C_FACE]], [wide], 16, emit)


def coarse_step_kernel(step, known, own, up, beside, coarse, table, flow, out, v1, v2, total):
    g = flow[0]
    gate = (g > 0).astype(jnp.float32)
    expand(up[...], row(table, C_LINK + 1), v1, gate)
    expand(beside[...], row(table, C_LINK + 2), v2)

    def emit_total(s, rows, tile):
        total[s, rows, :] = known[s, rows, :] + tile

    products([coarse.at[C_FACE + 1], coarse.at[C_FACE + 2]], [v1, v2], 16, emit_total)
    expand(total[...], lane_index() % 32, v1)
    sweep = jnp.broadcast_to(step - g, (8, LANES))

    def emit(s, rows, tile):
        fresh = jnp.where(sweep >= 0, tile, 0.0)
        out[s, rows, :] = jnp.where(sweep < SWEEPS, fresh, own[s, rows, :])

    products([coarse.at[C_INVERSE]], [v1], 16, emit)


def middle_up_local_kernel(r0, fix, middle, table, out, own, linked):
    place = row(table, M_POS)
    index, inside = chosen(place, lane_index() % 64, 0, 32)
    expand(-fix[...], index, own, inside)
    index, inside = chosen(place, row(table, M_LINK), 0, 32)
    expand(fix[...], index, linked, inside)

    def emit(s, rows, tile):
        out[s, rows, :] = r0[s, rows, :] + tile

    products([middle.at[M_DIAG], middle.at[M_FACE]], [own, linked], 32, emit)


def middle_up_kernel(
    known, f0, fix, up, beside, up_place, beside_place, middle, table, flow,
    out, v1, v2, total,
):
    gate = (flow[0] > 0).astype(jnp.float32)
    for v, got, places, k, scale in ((v1, up, up_place, 1, gate), (v2, beside, beside_place, 2, None)):
        place = places[64:72, :].astype(jnp.int32)[0:1]
        index, inside = chosen(place, row(table, M_LINK + k), 0, 32)
        expand(got[...], index, v, inside if scale is None else inside * scale)

    def emit_total(s, rows, tile):
        total[s, rows, :] = known[s, rows, :] + tile

    products([middle.at[M_FACE + 1], middle.at[M_FACE + 2]], [v1, v2], 32, emit_total)
    place = row(table, M_POS)
    index, inside = chosen(place, lane_index() % 64, 0, 32)
    expand(fix[...], index, v1, inside)
    out[...] = f0[...] + pack(v1[...], 2)
    expand(total[...], lane_index() % 64, v2)
    mask = (place >= 32).astype(jnp.float32)

    def emit(s, rows, tile):
        out[s, rows, :] += tile * mask

    products([middle.at[M_INVERSE]], [v2], 32, emit)


def fine_up_local_kernel(r0, fix, diag, faces, links, sent, out, own, linked):
    place = sent[128:136, :].astype(jnp.int32)[0:1]
    index, inside = chosen(place, lane_index(), 0, 64)
    expand(-fix[...], index, own, inside)
    index, inside = chosen(place, row(links, 0), 0, 64)
    expand(fix[...], index, linked, inside)

    def emit(s, rows, tile):
        out[s, rows, :] = r0[s, rows, :] + tile

    products([diag, faces.at[0]], [own, linked], B, emit)


def fine_up_kernel(
    known, f0, fix, up, beside, up_place, beside_place, faces, inverse, links, sent, flow,
    out, v1, v2, total,
):
    gate = (flow[0] > 0).astype(jnp.float32)
    for v, got, places, k, scale in ((v1, up, up_place, 1, gate), (v2, beside, beside_place, 2, None)):
        place = places[128:136, :].astype(jnp.int32)[0:1]
        index, inside = chosen(place, row(links, k), 0, 64)
        expand(got[...], index, v, inside if scale is None else inside * scale)

    def emit_total(s, rows, tile):
        total[s, rows, :] = known[s, rows, :] + tile

    products([faces.at[1], faces.at[2]], [v1, v2], B, emit_total)
    place = sent[128:136, :].astype(jnp.int32)[0:1]
    index, inside = chosen(place, lane_index(), 0, 64)
    expand(fix[...], index, v1, inside)
    mask = (place >= 64).astype(jnp.float32)

    def emit(s, rows, tile):
        out[s, rows, :] = f0[s, rows, :] + v1[s, rows, :] + tile * mask

    products([inverse], [total], B, emit)


WIDE = pltpu.VMEM((S, B, LANES), jnp.float32)


def f32(*shape):
    return jax.ShapeDtypeStruct(shape, jnp.float32)


def call(kernel, operands, outs, scratch=(), work=1.0, flow=None):
    specs = [pl.BlockSpec(memory_space=pltpu.VMEM)] * len(operands)
    if flow is not None:
        specs.append(pl.BlockSpec(memory_space=pltpu.SMEM))
        operands = (*operands, flow)
    return pl.pallas_call(
        kernel,
        out_shape=outs,
        in_specs=specs,
        out_specs=jax.tree.map(lambda _: pl.BlockSpec(memory_space=pltpu.VMEM), outs),
        scratch_shapes=list(scratch),
        compiler_params=pltpu.CompilerParams(vmem_limit_bytes=40 * 1024 * 1024),
        cost_estimate=pl.CostEstimate(
            flops=int(work * 4_000_000), bytes_accessed=int(work * 1_000_000), transcendentals=0
        ),
    )(*operands)


def from_behind(block, axis):
    size = lax.axis_size(axis)
    return lax.ppermute(block, axis, [(i, (i + 1) % size) for i in range(size)])


def own_part(array):
    return array[0, 0]


def shards(*arrays):
    (
        b, f_diag, f_inverse, f_faces, f_links, f_order, f_picks, f_weights,
        m_diag, m_inverse, m_faces, m_links, m_order, m_picks, m_weights,
        c_inverse, c_faces, c_links,
    ) = map(own_part, arrays)
    flow_size = lax.axis_size("flow")
    flow = lax.axis_index("flow").astype(jnp.int32).reshape(1)
    f_order = f_order.reshape(1, LANES)
    m_order = m_order.reshape(1, 64)

    f0, f_sent = call(start_kernel, (b, f_inverse, f_order), (f32(S, B, LANES), f32(136, LANES)))
    f_up, f_beside = from_behind(f_sent, "flow"), from_behind(f_sent, "tile")
    table, middle, coarse = call(
        prepare_kernel,
        (
            f_links, f_order, f_picks, m_links, m_order, m_picks, c_links,
            m_diag, m_inverse, m_faces, f_weights, c_inverse, c_faces, m_weights,
        ),
        (
            jax.ShapeDtypeStruct((TABLE, LANES), jnp.int32),
            jax.ShapeDtypeStruct((7, 32, B, LANES), jnp.bfloat16),
            jax.ShapeDtypeStruct((6, 16, B, LANES), jnp.bfloat16),
        ),
    )
    known = call(
        fine_local_kernel, (b, f0, f_diag, f_faces, f_links), f32(S, B, LANES), (WIDE, WIDE), 2.0
    )
    f_r0, right, m_f0, m_sent = call(
        fine_down_kernel,
        (known, f_up, f_beside, f_faces, table, middle),
        (f32(S, B, LANES), f32(S, 32, LANES), f32(S, 32, LANES), f32(72, LANES)),
        (WIDE, WIDE, WIDE),
        3.5,
        flow,
    )
    m_up, m_beside = from_behind(m_sent, "flow"), from_behind(m_sent, "tile")
    known = call(middle_local_kernel, (right, m_f0, middle, table), f32(S, 32, LANES), (WIDE, WIDE))
    m_r0, right, value = call(
        middle_down_kernel,
        (known, m_up, m_beside, middle, coarse, table),
        (f32(S, 32, LANES), f32(S, 16, LANES), f32(S, 16, LANES)),
        (WIDE, WIDE, WIDE),
        2.0,
        flow,
    )
    packed16 = pltpu.VMEM((S, 16, LANES), jnp.float32)
    for step in range(1, SWEEPS + flow_size - 1):
        up, beside = from_behind(value, "flow"), from_behind(value, "tile")
        known = call(coarse_local_kernel, (right, value, coarse, table), f32(S, 16, LANES), (WIDE,), 0.25)
        value = call(
            functools.partial(coarse_step_kernel, step),
            (known, value, up, beside, coarse, table),
            f32(S, 16, LANES),
            (WIDE, WIDE, packed16),
            0.75,
            flow,
        )
    beside = from_behind(value, "tile")
    known = call(middle_up_local_kernel, (m_r0, value, middle, table), f32(S, 32, LANES), (WIDE, WIDE))
    fix = call(
        middle_up_kernel,
        (known, m_f0, value, up, beside, m_up, m_beside, middle, table),
        f32(S, 32, LANES),
        (WIDE, WIDE, pltpu.VMEM((S, 32, LANES), jnp.float32)),
        1.5,
        flow,
    )
    up, beside = from_behind(fix, "flow"), from_behind(fix, "tile")
    known = call(
        fine_up_local_kernel,
        (f_r0, fix, f_diag, f_faces, f_links, f_sent),
        f32(S, B, LANES),
        (WIDE, WIDE),
        2.0,
    )
    field = call(
        fine_up_kernel,
        (known, f0, fix, up, beside, f_up, f_beside, f_faces, f_inverse, f_links, f_sent),
        f32(S, B, LANES),
        (WIDE, WIDE, WIDE),
        3.0,
        flow,
    )
    return field[None, None]


def solution(mesh):
    ranks = (5, 5, 5, 6, 4, 3, 4, 6, 5, 5, 6, 4, 3, 4, 6, 5, 6, 4)
    return jax.shard_map(
        shards,
        mesh=mesh,
        in_specs=tuple(P("flow", "tile", *[None] * (rank - 2)) for rank in ranks),
        out_specs=P("flow", "tile", None, None, None),
        check_vma=False,
    )
```

```python
import functools

import jax
import jax.numpy as jnp
from jax import lax
from jax.experimental import pallas as pl
from jax.experimental.pallas import tpu as pltpu
from jax.sharding import PartitionSpec as P

SWEEPS = 3
S = 4
B = 64
LANES = 128


F_LINK, F_PICK, F_COARSE, F_FINE = 0, 3, 5, 6
M_LINK, M_PICK, M_COARSE, M_FINE = 7, 10, 12, 13
C_LINK, M_POS, F_POS, TABLE = 14, 24, 32, 40


def lane_index():
    return lax.broadcasted_iota(jnp.int32, (1, LANES), 1)


def take_lanes(x, index):
    rows = x.reshape(-1, LANES)
    index = jnp.broadcast_to(index, rows.shape)
    return jnp.take_along_axis(rows, index, axis=1, mode="promise_in_bounds").reshape(x.shape)


def expand(packed, index, out, scale=None):
    rows = packed.shape[1]
    r = B // rows
    for h in range(r):
        values = take_lanes(packed, index + h * (LANES // r))
        if scale is not None:
            values = values * scale
        out[:, h * rows : (h + 1) * rows, :] = values


def pack(wide, r):
    rows = B // r
    group = lane_index() // (LANES // r)
    result = wide[:, :rows, :]
    for h in range(1, r):
        result = jnp.where(group == h, wide[:, h * rows : (h + 1) * rows, :], result)
    return result


def fold(parts):
    row = lax.broadcasted_iota(jnp.int32, (8, LANES), 0)
    high = row >= 4
    mid = (row & 2) > 0
    low = (row & 1) > 0
    level = []
    for i in range(4):
        a, b = parts[i], parts[i + 4]
        level.append(jnp.where(high, b, a) + pltpu.roll(jnp.where(high, a, b), 4, 0))
    pairs = []
    for i in range(2):
        a, b = level[i], level[i + 2]
        pairs.append(jnp.where(mid, b + pltpu.roll(b, 2, 0), a + pltpu.roll(a, 6, 0)))
    a, b = pairs
    return jnp.where(low, b + pltpu.roll(b, 1, 0), a + pltpu.roll(a, 7, 0))


def products(blocks, fields, rows, emit):
    def body(step, carry):
        base = pl.multiple_of(step * 8, 8)
        parts = [[None] * 8 for _ in range(S)]
        for block, field in zip(blocks, fields):
            for i in range(8):
                matrix = block[base + i].astype(jnp.float32)
                for s in range(S):
                    part = jnp.sum((matrix * field[s]).reshape(8, 8, LANES), axis=0)
                    parts[s][i] = part if parts[s][i] is None else parts[s][i] + part
        for s in range(S):
            emit(s, pl.ds(base, 8), fold(parts[s]))
        return carry

    lax.fori_loop(0, rows // 8, body, 0)


def positions(order, n):
    padded = order if n == LANES else jnp.where(lane_index() < n, order, -1)
    hit = padded == lax.broadcasted_iota(jnp.int32, (LANES, LANES), 0)
    place = lax.broadcasted_iota(jnp.int32, (8, LANES), 1).astype(jnp.float32)
    return lax.dot_general(
        place.astype(jnp.bfloat16),
        hit.astype(jnp.float32).astype(jnp.bfloat16),
        (((1,), (1,)), ((), ())),
        preferred_element_type=jnp.float32,
    )


CHUNKS = 4
SPARE = 8


def copy_out(sent, longer):
    rows = sent.shape[0]
    longer[0:rows, :] = sent[...]
    longer[rows : rows + SPARE, :] = jnp.zeros((SPARE, LANES), jnp.float32)


def copy_field(field, longer):
    rows = S * field.shape[1]
    longer[0:rows, :] = field[...].reshape(rows, LANES)
    longer[rows : rows + SPARE, :] = jnp.zeros((SPARE, LANES), jnp.float32)


def spread(values, n):
    return jnp.concatenate([values] * (LANES // n), axis=1)


def pick(source, index):
    source = jnp.broadcast_to(source, (8, LANES))
    return take_lanes(source, jnp.broadcast_to(index, (8, LANES)))[0:1]


def fill_table(f_links, f_order, f_picks, m_links, m_order, m_picks, c_links, table):
    lane = lane_index()

    def put(place, values):
        table[place : place + 1, :] = values

    for k in range(3):
        put(F_LINK + k, f_links[k])
        put(M_LINK + k, spread(m_links[k], 64))
        put(C_LINK + k, spread(c_links[k], 32))
    order = f_order[...]
    wide_order = spread(m_order[...], 64)
    for k in range(2):
        put(F_PICK + k, pick(order, 64 + spread(f_picks[k : k + 1, :], 64)))
        put(M_PICK + k, pick(wide_order, 32 + spread(m_picks[k : k + 1, :], 32)))
    put(F_COARSE, pick(order, lane % 64))
    put(F_FINE, pick(order, 64 + lane % 64))
    put(M_COARSE, pick(wide_order, lane % 32))
    put(M_FINE, pick(wide_order, 32 + lane % 32))
    place = positions(wide_order, 64).astype(jnp.int32)
    table[M_POS:F_POS, :] = take_lanes(place, lane % 64)
    table[F_POS:TABLE, :] = positions(order, LANES).astype(jnp.int32)


def start_kernel(*refs):
    sources, (f0, sent, longer, table) = refs[:9], refs[9:13]
    held, semaphores = refs[13:22], refs[22]
    b, inverse = held[:2]
    rows = B // CHUNKS
    copies = [pltpu.make_async_copy(sources[k], held[k], semaphores.at[k]) for k in (2, 3, 4, 5, 6, 7, 8, 0)]
    parts = []
    for c in range(CHUNKS):
        part = pl.ds(c * rows, rows)
        parts.append(pltpu.make_async_copy(sources[1].at[part], inverse.at[part], semaphores.at[9 + c]))
    for copy in copies + parts:
        copy.start()
    for copy in copies[:7]:
        copy.wait()
    fill_table(*held[2:], table)
    mask = (row(table, F_POS) >= 64).astype(jnp.float32)
    copies[7].wait()
    for c in range(CHUNKS):
        parts[c].wait()

        def emit(s, at, tile):
            f0[s, pl.ds(pl.multiple_of(c * rows + at.start, 8), 8), :] = tile * mask

        products([inverse.at[pl.ds(c * rows, rows)]], [b], rows, emit)
    wide = take_lanes(f0[...], row(table, F_FINE))
    sent[0:128, :] = pack(wide, 2).reshape(128, LANES)
    sent[128:136, :] = table[F_POS:TABLE, :].astype(jnp.float32)
    copy_out(sent, longer)


def place_lanes(n, offset):
    shape = (n, LANES)
    source = lax.broadcasted_iota(jnp.int32, shape, 0)
    hit = lax.broadcasted_iota(jnp.int32, shape, 1) == source + offset
    return hit.astype(jnp.float32).astype(jnp.bfloat16)


def dot(a, b, contract):
    return lax.dot_general(a, b, (contract, ((), ())), preferred_element_type=jnp.float32)


def pack_halves(sources, out):
    low, high = place_lanes(64, 0), place_lanes(64, 64)

    def body(step, carry):
        base = pl.multiple_of(step * 8, 8)
        for slot, source in enumerate(sources):
            first = source[pl.ds(base, 8)].reshape(8 * B, 64)
            second = source[pl.ds(base + 32, 8)].reshape(8 * B, 64)
            both = dot(first, low, ((1,), (0,))) + dot(second, high, ((1,), (0,)))
            out[slot, pl.ds(base, 8)] = both.astype(jnp.bfloat16).reshape(8, B, LANES)
        return carry

    lax.fori_loop(0, 4, body, 0)


def pack_quarters(sources, out):
    unit = place_lanes(64, 0)[:, :64]

    def body(step, carry):
        for slot, source in enumerate(sources):
            for k in range(4):
                i = step * 4 + k
                points = jnp.concatenate([source[16 * q + i] for q in range(4)], axis=0)
                out[slot, i] = dot(unit, points, ((1,), (1,))).astype(jnp.bfloat16)
        return carry

    lax.fori_loop(0, 4, body, 0)


def select_fine(sources, table, out):
    source = lax.broadcasted_iota(jnp.int32, (LANES, LANES), 0)
    hit = source == jnp.broadcast_to(row(table, F_FINE), (LANES, LANES))
    first = lax.broadcasted_iota(jnp.int32, (LANES, LANES), 1) < 64
    low = jnp.where(hit & first, 1.0, 0.0).astype(jnp.bfloat16)
    high = jnp.where(hit & ~first, 1.0, 0.0).astype(jnp.bfloat16)

    def body(step, carry):
        base = pl.multiple_of(step * 8, 8)
        for slot, source in enumerate(sources):
            a = source[pl.ds(base, 8)].reshape(8 * B, LANES)
            b = source[pl.ds(base + 32, 8)].reshape(8 * B, LANES)
            both = dot(a, low, ((1,), (0,))) + dot(b, high, ((1,), (0,)))
            out[slot, pl.ds(base, 8)] = both.astype(jnp.bfloat16).reshape(8, B, LANES)
        return carry

    lax.fori_loop(0, 4, body, 0)


def select_middle(sources, table, out):
    source = lax.broadcasted_iota(jnp.int32, (LANES, LANES), 0)
    group = lax.broadcasted_iota(jnp.int32, (LANES, LANES), 1) // 32
    hit = source == jnp.broadcast_to(row(table, M_FINE), (LANES, LANES)) + 64 * (group // 2)
    low = jnp.where(hit & (group % 2 == 0), 1.0, 0.0).astype(jnp.bfloat16)
    high = jnp.where(hit & (group % 2 == 1), 1.0, 0.0).astype(jnp.bfloat16)

    def body(step, carry):
        base = pl.multiple_of(step * 8, 8)
        for slot, source in enumerate(sources):
            a = source[pl.ds(base, 8)].reshape(8 * B, LANES)
            b = source[pl.ds(base + 16, 8)].reshape(8 * B, LANES)
            both = dot(a, low, ((1,), (0,))) + dot(b, high, ((1,), (0,)))
            out[slot, pl.ds(base, 8)] = both.astype(jnp.bfloat16).reshape(8, B, LANES)
        return carry

    lax.fori_loop(0, 2, body, 0)


M_INVERSE, F_WEIGHT = 0, 1
M_DIAG, M_FACE = 0, 1
C_INVERSE, M_WEIGHT = 0, 1


def row(table, k):
    return table[k : k + 1, :]


def fine_local_kernel(
    b_hbm, f0_hbm, diag_hbm, faces_hbm, table_hbm, m_inverse_hbm, f_weights_hbm, out, first,
    b, f0, diag, face, table, m_inverse, f_weights, semaphores, own, linked,
):
    sources = [f0_hbm, table_hbm, diag_hbm, faces_hbm.at[0], b_hbm, m_inverse_hbm, f_weights_hbm]
    targets = [f0, table, diag, face, b, m_inverse, f_weights]
    copies = [pltpu.make_async_copy(x, y, semaphores.at[k]) for k, (x, y) in enumerate(zip(sources, targets))]
    for copy in copies:
        copy.start()
    for copy in copies[:5]:
        copy.wait()
    own[...] = -f0[...]
    linked[...] = take_lanes(f0[...], row(table, F_LINK))

    def emit(s, rows, tile):
        out[s, rows, :] = b[s, rows, :] + tile

    products([diag, face], [own, linked], B, emit)
    for copy in copies[5:]:
        copy.wait()
    pack_halves([m_inverse, f_weights.at[0], f_weights.at[1]], first)


def chosen(place, index, low, high):
    spot = take_lanes(jnp.broadcast_to(place, (8, LANES)), jnp.broadcast_to(index, (8, LANES)))[0:1]
    inside = (spot >= low) & (spot < high)
    return jnp.clip(spot - low, 0, high - low - 1), inside.astype(jnp.float32)


def gate_of(flow):
    return (flow[0] > 0).astype(jnp.float32)


def fine_flow_kernel(known, up, faces, table, flow, out, v):
    index, inside = chosen(up[128:136, :].astype(jnp.int32)[0:1], row(table, F_LINK + 1), 64, 128)
    expand(up[0:128, :].reshape(S, 32, LANES), index, v, inside * gate_of(flow))

    def emit(s, rows, tile):
        out[s, rows, :] = known[s, rows, :] + tile

    products([faces.at[1]], [v], B, emit)


def fine_down_kernel(
    known, beside, faces, table, first,
    r0, right, f0, sent, longer, v1, v2, wide,
):
    index, inside = chosen(beside[128:136, :].astype(jnp.int32)[0:1], row(table, F_LINK + 2), 64, 128)
    expand(beside[0:128, :].reshape(S, 32, LANES), index, v2, inside)

    def emit_residual(s, rows, tile):
        r0[s, rows, :] = known[s, rows, :] + tile

    products([faces.at[2]], [v2], B, emit_residual)
    residual = r0[...]
    v1[...] = take_lanes(residual, row(table, F_PICK))
    v2[...] = take_lanes(residual, row(table, F_PICK + 1))
    wide[...] = take_lanes(residual, row(table, F_COARSE))
    right[...] = pack(wide[...], 2)

    def emit_right(s, rows, tile):
        right[s, rows, :] += tile

    products([first.at[F_WEIGHT], first.at[F_WEIGHT + 1]], [v1, v2], 32, emit_right)
    expand(right[...], lane_index() % 64, wide)
    mask = (row(table, M_POS) >= 32).astype(jnp.float32)

    def emit_field(s, rows, tile):
        f0[s, rows, :] = tile * mask

    products([first.at[M_INVERSE]], [wide], 32, emit_field)
    expand(f0[...], row(table, M_FINE), wide)
    sent[0:64, :] = pack(wide[...], 4).reshape(64, LANES)
    sent[64:72, :] = table[M_POS:F_POS, :].astype(jnp.float32)
    copy_out(sent, longer)


def middle_local_kernel(
    b, f0, table, m_diag, m_faces, c_inverse, m_weights, out, middle, coarse, own, linked
):
    pack_halves([m_diag, m_faces.at[0], m_faces.at[1], m_faces.at[2]], middle)
    pack_quarters([c_inverse, m_weights.at[0], m_weights.at[1]], coarse)
    expand(-f0[...], lane_index() % 64, own)
    expand(f0[...], row(table, M_LINK), linked)

    def emit(s, rows, tile):
        out[s, rows, :] = b[s, rows, :] + tile

    products([middle.at[M_DIAG], middle.at[M_FACE]], [own, linked], 32, emit)


def middle_flow_kernel(known, up, middle, table, flow, out, v):
    index, inside = chosen(up[64:72, :].astype(jnp.int32)[0:1], row(table, M_LINK + 1), 32, 64)
    expand(up[0:64, :].reshape(S, 16, LANES), index, v, inside * gate_of(flow))

    def emit(s, rows, tile):
        out[s, rows, :] = known[s, rows, :] + tile

    products([middle.at[M_FACE + 1]], [v], 32, emit)


def middle_down_kernel(
    known, beside, middle, coarse, table, flow,
    r0, right, first, longer, v1, v2, wide,
):
    index, inside = chosen(beside[64:72, :].astype(jnp.int32)[0:1], row(table, M_LINK + 2), 32, 64)
    expand(beside[0:64, :].reshape(S, 16, LANES), index, v2, inside)

    def emit_residual(s, rows, tile):
        r0[s, rows, :] = known[s, rows, :] + tile

    products([middle.at[M_FACE + 2]], [v2], 32, emit_residual)
    residual = r0[...]
    expand(residual, row(table, M_PICK), v1)
    expand(residual, row(table, M_PICK + 1), v2)
    expand(residual, row(table, M_COARSE), wide)
    right[...] = pack(wide[...], 4)

    def emit_right(s, rows, tile):
        right[s, rows, :] += tile

    products([coarse.at[M_WEIGHT], coarse.at[M_WEIGHT + 1]], [v1, v2], 16, emit_right)
    expand(right[...], lane_index() % 32, wide)
    start = (flow[0] == 0).astype(jnp.float32)

    def emit_first(s, rows, tile):
        first[s, rows, :] = tile * start

    products([coarse.at[C_INVERSE]], [wide], 16, emit_first)
    copy_field(first, longer)


def coarse_first_kernel(right, own, c_faces, table, out, faces, wide):
    pack_quarters([c_faces.at[0], c_faces.at[1], c_faces.at[2]], faces)
    coarse_local_kernel(right, own, faces, table, out, wide)


def coarse_fine_kernel(right, own, faces, table, f_inverse, f_faces, out, chosen_fine, wide):
    select_fine([f_inverse, f_faces.at[1], f_faces.at[2]], table, chosen_fine)
    coarse_local_kernel(right, own, faces, table, out, wide)


def coarse_middle_kernel(right, own, faces, table, first, middle, out, chosen_middle, wide):
    sources = [first.at[M_INVERSE], middle.at[M_FACE + 1], middle.at[M_FACE + 2]]
    select_middle(sources, table, chosen_middle)
    coarse_local_kernel(right, own, faces, table, out, wide)


def coarse_local_kernel(right, own, faces, table, out, wide):
    expand(own[...], row(table, C_LINK), wide)

    def emit(s, rows, tile):
        out[s, rows, :] = right[s, rows, :] + tile

    products([faces.at[0]], [wide], 16, emit)


def coarse_flow_kernel(known, up, faces, table, flow, out, v):
    expand(up[...], row(table, C_LINK + 1), v, gate_of(flow))

    def emit(s, rows, tile):
        out[s, rows, :] = known[s, rows, :] + tile

    products([faces.at[1]], [v], 16, emit)


def coarse_step_kernel(step, known, own, beside, coarse, faces, table, flow, out, longer, v1, v2, total):
    expand(beside[0:64, :].reshape(S, 16, LANES), row(table, C_LINK + 2), v2)

    def emit_total(s, rows, tile):
        total[s, rows, :] = known[s, rows, :] + tile

    products([faces.at[2]], [v2], 16, emit_total)
    expand(total[...], lane_index() % 32, v1)
    sweep = jnp.broadcast_to(step - flow[0], (8, LANES))

    def emit(s, rows, tile):
        fresh = jnp.where(sweep >= 0, tile, 0.0)
        out[s, rows, :] = jnp.where(sweep < SWEEPS, fresh, own[s, rows, :])

    products([coarse.at[C_INVERSE]], [v1], 16, emit)
    copy_field(out, longer)


def middle_up_local_kernel(r0, f0, fix, up, up_place, middle, chosen_middle, table, flow, out, base, own, linked, known):
    place = row(table, M_POS)
    index, inside = chosen(place, lane_index() % 64, 0, 32)
    expand(fix[...], index, own, inside)
    base[...] = f0[...] + pack(own[...], 2)
    own[...] = -own[...]
    index, inside = chosen(place, row(table, M_LINK), 0, 32)
    expand(fix[...], index, linked, inside)

    def emit(s, rows, tile):
        known[s, rows, :] = r0[s, rows, :] + tile

    products([middle.at[M_DIAG], middle.at[M_FACE]], [own, linked], 32, emit)
    expand(known[...], row(table, M_FINE), own)
    link = pick(row(table, M_LINK + 1), row(table, M_FINE))
    index, inside = chosen(up_place[64:72, :].astype(jnp.int32)[0:1], link, 0, 32)
    expand(up[...], index, linked, inside * gate_of(flow))
    out[...] = pack(own[...], 4)

    def emit_flow(s, rows, tile):
        out[s, rows, :] += tile

    products([chosen_middle.at[1]], [linked], 16, emit_flow)


def middle_up_kernel(known, base, beside, beside_place, chosen_middle, table, out, longer, v1, v2, total, result):
    link = pick(row(table, M_LINK + 2), row(table, M_FINE))
    index, inside = chosen(beside_place[64:72, :].astype(jnp.int32)[0:1], link, 0, 32)
    expand(beside[...], index, v1, inside)

    def emit_total(s, rows, tile):
        total[s, rows, :] = known[s, rows, :] + tile

    products([chosen_middle.at[2]], [v1], 16, emit_total)
    expand(total[...], lane_index() % 32, v2)

    def emit(s, rows, tile):
        result[s, rows, :] = tile

    products([chosen_middle.at[0]], [v2], 16, emit)
    index, inside = chosen(row(table, M_POS), lane_index() % 64, 32, 64)
    expand(result[...], index, v1, inside)
    out[...] = base[...] + pack(v1[...], 2)
    copy_field(out, longer)


def fine_up_local_kernel(r0, f0, fix, diag, faces, table, out, base, own, linked, known):
    place = row(table, F_POS)
    index, inside = chosen(place, lane_index(), 0, 64)
    expand(fix[...], index, own, inside)
    base[...] = f0[...] + own[...]
    own[...] = -own[...]
    index, inside = chosen(place, row(table, F_LINK), 0, 64)
    expand(fix[...], index, linked, inside)

    def emit(s, rows, tile):
        known[s, rows, :] = r0[s, rows, :] + tile

    products([diag, faces.at[0]], [own, linked], B, emit)
    own[...] = take_lanes(known[...], row(table, F_FINE))
    out[...] = pack(own[...], 2)


def fine_up_flow_kernel(known, up, up_place, chosen_fine, table, flow, out, v):
    link = pick(row(table, F_LINK + 1), row(table, F_FINE))
    index, inside = chosen(up_place[128:136, :].astype(jnp.int32)[0:1], link, 0, 64)
    expand(up[...], index, v, inside * gate_of(flow))

    def emit(s, rows, tile):
        out[s, rows, :] = known[s, rows, :] + tile

    products([chosen_fine.at[1]], [v], 32, emit)


def fine_up_kernel(known, base, beside, beside_place, chosen_fine, table, out, v1, v2, total, result):
    link = pick(row(table, F_LINK + 2), row(table, F_FINE))
    index, inside = chosen(beside_place[128:136, :].astype(jnp.int32)[0:1], link, 0, 64)
    expand(beside[0:128, :].reshape(S, 32, LANES), index, v1, inside)

    def emit_total(s, rows, tile):
        total[s, rows, :] = known[s, rows, :] + tile

    products([chosen_fine.at[2]], [v1], 32, emit_total)
    expand(total[...], lane_index() % 64, v2)

    def emit(s, rows, tile):
        result[s, rows, :] = tile

    products([chosen_fine.at[0]], [v2], 32, emit)
    index, inside = chosen(row(table, F_POS), lane_index(), 64, 128)
    expand(result[...], index, v1, inside)
    out[...] = base[...] + v1[...]


WIDE = pltpu.VMEM((S, B, LANES), jnp.float32)


def f32(*shape):
    return jax.ShapeDtypeStruct(shape, jnp.float32)


def bf16(*shape):
    return jax.ShapeDtypeStruct(shape, jnp.bfloat16)


def call(kernel, operands, outs, scratch=(), work=1.0, flow=None, space=pltpu.VMEM, limit=40 * 1024):
    specs = [pl.BlockSpec(memory_space=space)] * len(operands)
    if flow is not None:
        specs.append(pl.BlockSpec(memory_space=pltpu.SMEM))
        operands = (*operands, flow)
    return pl.pallas_call(
        kernel,
        out_shape=outs,
        in_specs=specs,
        out_specs=jax.tree.map(lambda _: pl.BlockSpec(memory_space=pltpu.VMEM), outs),
        scratch_shapes=list(scratch),
        compiler_params=pltpu.CompilerParams(vmem_limit_bytes=limit * 1024),
        cost_estimate=pl.CostEstimate(
            flops=int(work * 4_000_000), bytes_accessed=int(work * 1_000_000), transcendentals=0
        ),
    )(*operands)


def from_behind(block, axis):
    size = lax.axis_size(axis)
    return lax.ppermute(block, axis, [(i, (i + 1) % size) for i in range(size)])


def own_part(array):
    return array[0, 0]


def shards(*arrays):
    (
        b, f_diag, f_inverse, f_faces, f_links, f_order, f_picks, f_weights,
        m_diag, m_inverse, m_faces, m_links, m_order, m_picks, m_weights,
        c_inverse, c_faces, c_links,
    ) = map(own_part, arrays)
    flow_size = lax.axis_size("flow")
    flow = lax.axis_index("flow").astype(jnp.int32).reshape(1)
    f_order = f_order.reshape(1, LANES)
    m_order = m_order.reshape(1, 64)
    f_links, m_links, c_links = (x.reshape(3, 1, -1) for x in (f_links, m_links, c_links))
    c_inverse, c_faces, m_weights = (jnp.swapaxes(x, -1, -2) for x in (c_inverse, c_faces, m_weights))

    f0, f_sent, f_longer, table = call(
        start_kernel,
        (b, f_inverse, f_links, f_order, f_picks, m_links, m_order, m_picks, c_links),
        (
            f32(S, B, LANES), f32(136, LANES), f32(136 + SPARE, LANES),
            jax.ShapeDtypeStruct((TABLE, LANES), jnp.int32),
        ),
        (
            WIDE,
            pltpu.VMEM((B, B, LANES), jnp.bfloat16),
            *[pltpu.VMEM(x.shape, jnp.int32) for x in (f_links, f_order, f_picks, m_links, m_order, m_picks, c_links)],
            pltpu.SemaphoreType.DMA((9 + CHUNKS,)),
        ),
        space=pltpu.HBM,
        limit=65000,
    )
    f_beside, f_up = from_behind(f_longer, "tile"), from_behind(f_sent, "flow")
    known, first = call(
        fine_local_kernel,
        (b, f0, f_diag, f_faces, table, m_inverse, f_weights),
        (f32(S, B, LANES), bf16(3, 32, B, LANES)),
        (
            WIDE,
            WIDE,
            pltpu.VMEM((B, B, LANES), jnp.bfloat16),
            pltpu.VMEM((B, B, LANES), jnp.bfloat16),
            pltpu.VMEM((TABLE, LANES), jnp.int32),
            pltpu.VMEM(m_inverse.shape, jnp.bfloat16),
            pltpu.VMEM(f_weights.shape, jnp.bfloat16),
            pltpu.SemaphoreType.DMA((7,)),
            WIDE,
            WIDE,
        ),
        3.0,
        space=pltpu.HBM,
        limit=56000,
    )
    known = call(fine_flow_kernel, (known, f_up, f_faces, table), f32(S, B, LANES), (WIDE,), 0.0, flow)
    f_r0, right, m_f0, m_sent, m_longer = call(
        fine_down_kernel,
        (known, f_beside, f_faces, table, first),
        (f32(S, B, LANES), f32(S, 32, LANES), f32(S, 32, LANES), f32(72, LANES), f32(72 + SPARE, LANES)),
        (WIDE, WIDE, WIDE),
        2.5,
    )
    m_beside, m_up = from_behind(m_longer, "tile"), from_behind(m_sent, "flow")
    known, middle, coarse = call(
        middle_local_kernel,
        (right, m_f0, table, m_diag, m_faces, c_inverse, m_weights),
        (f32(S, 32, LANES), bf16(4, 32, B, LANES), bf16(3, 16, B, LANES)),
        (WIDE, WIDE),
        2.0,
    )
    known = call(middle_flow_kernel, (known, m_up, middle, table), f32(S, 32, LANES), (WIDE,), 0.0, flow)
    m_r0, right, value, longer = call(
        middle_down_kernel,
        (known, m_beside, middle, coarse, table),
        (f32(S, 32, LANES), f32(S, 16, LANES), f32(S, 16, LANES), f32(64 + SPARE, LANES)),
        (WIDE, WIDE, WIDE),
        1.5,
        flow,
    )
    packed16 = pltpu.VMEM((S, 16, LANES), jnp.float32)
    packed32 = pltpu.VMEM((S, 32, LANES), jnp.float32)
    for step in range(1, SWEEPS + flow_size - 1):
        beside, up = from_behind(longer, "tile"), from_behind(value, "flow")
        if step == 1:
            known, faces = call(
                coarse_first_kernel,
                (right, value, c_faces, table),
                (f32(S, 16, LANES), bf16(3, 16, B, LANES)),
                (WIDE,),
            )
        elif step == 2:
            known, chosen_fine = call(
                coarse_fine_kernel,
                (right, value, faces, table, f_inverse, f_faces),
                (f32(S, 16, LANES), bf16(3, 32, B, LANES)),
                (WIDE,),
            )
        elif step == 3:
            known, chosen_middle = call(
                coarse_middle_kernel,
                (right, value, faces, table, first, middle),
                (f32(S, 16, LANES), bf16(3, 16, B, LANES)),
                (WIDE,),
            )
        else:
            known = call(coarse_local_kernel, (right, value, faces, table), f32(S, 16, LANES), (WIDE,), 0.25)
        known = call(coarse_flow_kernel, (known, up, faces, table), f32(S, 16, LANES), (WIDE,), 0.0, flow)
        value, longer = call(
            functools.partial(coarse_step_kernel, step),
            (known, value, beside, coarse, faces, table),
            (f32(S, 16, LANES), f32(64 + SPARE, LANES)),
            (WIDE, WIDE, packed16),
            0.5,
            flow,
        )
    beside = from_behind(value, "tile")
    known, base = call(
        middle_up_local_kernel,
        (m_r0, m_f0, value, up, m_up, middle, chosen_middle, table),
        (f32(S, 16, LANES), f32(S, 32, LANES)),
        (WIDE, WIDE, packed32),
        1.25,
        flow,
    )
    fix, longer = call(
        middle_up_kernel,
        (known, base, beside, m_beside, chosen_middle, table),
        (f32(S, 32, LANES), f32(128 + SPARE, LANES)),
        (WIDE, WIDE, packed16, packed16),
        0.5,
    )
    beside, up = from_behind(longer, "tile"), from_behind(fix, "flow")
    known, base = call(
        fine_up_local_kernel,
        (f_r0, f0, fix, f_diag, f_faces, table),
        (f32(S, 32, LANES), f32(S, B, LANES)),
        (WIDE, WIDE, WIDE),
        2.0,
    )
    known = call(fine_up_flow_kernel, (known, up, f_up, chosen_fine, table), f32(S, 32, LANES), (WIDE,), 0.0, flow)
    field = call(
        fine_up_kernel,
        (known, base, beside, f_beside, chosen_fine, table),
        f32(S, B, LANES),
        (WIDE, WIDE, packed32, packed32),
        1.0,
    )
    return field[None, None]


def solution(mesh):
    ranks = (5, 5, 5, 6, 4, 3, 4, 6, 5, 5, 6, 4, 3, 4, 6, 5, 6, 4)
    return jax.shard_map(
        shards,
        mesh=mesh,
        in_specs=tuple(P("flow", "tile", *[None] * (rank - 2)) for rank in ranks),
        out_specs=P("flow", "tile", None, None, None),
        check_vma=False,
    )
```

```python
import functools

import jax
import jax.numpy as jnp
from jax import lax
from jax.experimental import pallas as pl
from jax.experimental.pallas import tpu as pltpu
from jax.sharding import PartitionSpec as P

SWEEPS = 3
S = 4
B = 64
LANES = 128


F_LINK, F_PICK, F_COARSE, F_FINE = 0, 3, 5, 6
M_LINK, M_PICK, M_COARSE, M_FINE = 7, 10, 12, 13
C_LINK, M_POS, F_POS, TABLE = 14, 24, 32, 40


def lane_index():
    return lax.broadcasted_iota(jnp.int32, (1, LANES), 1)


def take_lanes(x, index):
    rows = x.reshape(-1, LANES)
    index = jnp.broadcast_to(index, rows.shape)
    return jnp.take_along_axis(rows, index, axis=1, mode="promise_in_bounds").reshape(x.shape)


def expand(packed, index, out, scale=None):
    rows = packed.shape[1]
    r = B // rows
    for h in range(r):
        values = take_lanes(packed, index + h * (LANES // r))
        if scale is not None:
            values = values * scale
        out[:, h * rows : (h + 1) * rows, :] = values


def pack(wide, r):
    rows = B // r
    group = lane_index() // (LANES // r)
    result = wide[:, :rows, :]
    for h in range(1, r):
        result = jnp.where(group == h, wide[:, h * rows : (h + 1) * rows, :], result)
    return result


def fold(parts):
    row = lax.broadcasted_iota(jnp.int32, (8, LANES), 0)
    high = row >= 4
    mid = (row & 2) > 0
    low = (row & 1) > 0
    level = []
    for i in range(4):
        a, b = parts[i], parts[i + 4]
        level.append(jnp.where(high, b, a) + pltpu.roll(jnp.where(high, a, b), 4, 0))
    pairs = []
    for i in range(2):
        a, b = level[i], level[i + 2]
        pairs.append(jnp.where(mid, b + pltpu.roll(b, 2, 0), a + pltpu.roll(a, 6, 0)))
    a, b = pairs
    return jnp.where(low, b + pltpu.roll(b, 1, 0), a + pltpu.roll(a, 7, 0))


def products(blocks, fields, rows, emit):
    def body(step, carry):
        base = pl.multiple_of(step * 8, 8)
        parts = [[None] * 8 for _ in range(S)]
        for block, field in zip(blocks, fields):
            for i in range(8):
                matrix = block[base + i].astype(jnp.float32)
                for s in range(S):
                    part = jnp.sum((matrix * field[s]).reshape(8, 8, LANES), axis=0)
                    parts[s][i] = part if parts[s][i] is None else parts[s][i] + part
        for s in range(S):
            emit(s, pl.ds(base, 8), fold(parts[s]))
        return carry

    lax.fori_loop(0, rows // 8, body, 0)


def positions(order, n):
    padded = order if n == LANES else jnp.where(lane_index() < n, order, -1)
    hit = padded == lax.broadcasted_iota(jnp.int32, (LANES, LANES), 0)
    place = lax.broadcasted_iota(jnp.int32, (8, LANES), 1).astype(jnp.float32)
    return lax.dot_general(
        place.astype(jnp.bfloat16),
        hit.astype(jnp.float32).astype(jnp.bfloat16),
        (((1,), (1,)), ((), ())),
        preferred_element_type=jnp.float32,
    )


CHUNKS = 4
SPARE = 8


def copy_out(sent, longer):
    rows = sent.shape[0]
    longer[0:rows, :] = sent[...]
    longer[rows : rows + SPARE, :] = jnp.zeros((SPARE, LANES), jnp.float32)


def copy_field(field, longer):
    rows = S * field.shape[1]
    longer[0:rows, :] = field[...].reshape(rows, LANES)
    longer[rows : rows + SPARE, :] = jnp.zeros((SPARE, LANES), jnp.float32)


def spread(values, n):
    return jnp.concatenate([values] * (LANES // n), axis=1)


def pick(source, index):
    source = jnp.broadcast_to(source, (8, LANES))
    return take_lanes(source, jnp.broadcast_to(index, (8, LANES)))[0:1]


def fill_table(f_links, f_order, f_picks, m_links, m_order, m_picks, c_links, table):
    lane = lane_index()

    def put(place, values):
        table[place : place + 1, :] = values

    for k in range(3):
        put(F_LINK + k, f_links[k])
        put(M_LINK + k, spread(m_links[k], 64))
        put(C_LINK + k, spread(c_links[k], 32))
    order = f_order[...]
    wide_order = spread(m_order[...], 64)
    for k in range(2):
        put(F_PICK + k, pick(order, 64 + spread(f_picks[k : k + 1, :], 64)))
        put(M_PICK + k, pick(wide_order, 32 + spread(m_picks[k : k + 1, :], 32)))
    put(F_COARSE, pick(order, lane % 64))
    put(F_FINE, pick(order, 64 + lane % 64))
    put(M_COARSE, pick(wide_order, lane % 32))
    put(M_FINE, pick(wide_order, 32 + lane % 32))
    place = positions(wide_order, 64).astype(jnp.int32)
    table[M_POS:F_POS, :] = take_lanes(place, lane % 64)
    table[F_POS:TABLE, :] = positions(order, LANES).astype(jnp.int32)


def start_kernel(*refs):
    sources, (f0, linked, sent, longer, table) = refs[:9], refs[9:14]
    held, semaphores = refs[14:23], refs[23]
    b, inverse = held[:2]
    rows = B // CHUNKS
    copies = [pltpu.make_async_copy(sources[k], held[k], semaphores.at[k]) for k in (2, 3, 4, 5, 6, 7, 8, 0)]
    parts = []
    for c in range(CHUNKS):
        part = pl.ds(c * rows, rows)
        parts.append(pltpu.make_async_copy(sources[1].at[part], inverse.at[part], semaphores.at[9 + c]))
    for copy in copies + parts:
        copy.start()
    for copy in copies[:7]:
        copy.wait()
    fill_table(*held[2:], table)
    mask = (row(table, F_POS) >= 64).astype(jnp.float32)
    copies[7].wait()
    for c in range(CHUNKS):
        parts[c].wait()

        def emit(s, at, tile):
            f0[s, pl.ds(pl.multiple_of(c * rows + at.start, 8), 8), :] = tile * mask

        products([inverse.at[pl.ds(c * rows, rows)]], [b], rows, emit)
    wide = take_lanes(f0[...], row(table, F_FINE))
    sent[0:128, :] = pack(wide, 2).reshape(128, LANES)
    sent[128:136, :] = table[F_POS:TABLE, :].astype(jnp.float32)
    copy_out(sent, longer)
    linked[...] = take_lanes(f0[...], row(table, F_LINK))


def place_lanes(n, offset):
    shape = (n, LANES)
    source = lax.broadcasted_iota(jnp.int32, shape, 0)
    hit = lax.broadcasted_iota(jnp.int32, shape, 1) == source + offset
    return hit.astype(jnp.float32).astype(jnp.bfloat16)


def dot(a, b, contract):
    return lax.dot_general(a, b, (contract, ((), ())), preferred_element_type=jnp.float32)


def pack_halves(sources, out):
    low, high = place_lanes(64, 0), place_lanes(64, 64)

    def body(step, carry):
        base = pl.multiple_of(step * 8, 8)
        for slot, source in enumerate(sources):
            first = source[pl.ds(base, 8)].reshape(8 * B, 64)
            second = source[pl.ds(base + 32, 8)].reshape(8 * B, 64)
            both = dot(first, low, ((1,), (0,))) + dot(second, high, ((1,), (0,)))
            out[slot, pl.ds(base, 8)] = both.astype(jnp.bfloat16).reshape(8, B, LANES)
        return carry

    lax.fori_loop(0, 4, body, 0)


def pack_quarters(sources, out):
    unit = place_lanes(64, 0)[:, :64]

    def body(step, carry):
        for slot, source in enumerate(sources):
            for k in range(4):
                i = step * 4 + k
                points = jnp.concatenate([source[16 * q + i] for q in range(4)], axis=0)
                out[slot, i] = dot(unit, points, ((1,), (1,))).astype(jnp.bfloat16)
        return carry

    lax.fori_loop(0, 4, body, 0)


def select_fine(sources, table, out):
    source = lax.broadcasted_iota(jnp.int32, (LANES, LANES), 0)
    hit = source == jnp.broadcast_to(row(table, F_FINE), (LANES, LANES))
    first = lax.broadcasted_iota(jnp.int32, (LANES, LANES), 1) < 64
    low = jnp.where(hit & first, 1.0, 0.0).astype(jnp.bfloat16)
    high = jnp.where(hit & ~first, 1.0, 0.0).astype(jnp.bfloat16)

    def body(step, carry):
        base = pl.multiple_of(step * 8, 8)
        for slot, source in enumerate(sources):
            a = source[pl.ds(base, 8)].reshape(8 * B, LANES)
            b = source[pl.ds(base + 32, 8)].reshape(8 * B, LANES)
            both = dot(a, low, ((1,), (0,))) + dot(b, high, ((1,), (0,)))
            out[slot, pl.ds(base, 8)] = both.astype(jnp.bfloat16).reshape(8, B, LANES)
        return carry

    lax.fori_loop(0, 4, body, 0)


def select_middle(sources, table, out):
    source = lax.broadcasted_iota(jnp.int32, (LANES, LANES), 0)
    group = lax.broadcasted_iota(jnp.int32, (LANES, LANES), 1) // 32
    hit = source == jnp.broadcast_to(row(table, M_FINE), (LANES, LANES)) + 64 * (group // 2)
    low = jnp.where(hit & (group % 2 == 0), 1.0, 0.0).astype(jnp.bfloat16)
    high = jnp.where(hit & (group % 2 == 1), 1.0, 0.0).astype(jnp.bfloat16)

    def body(step, carry):
        base = pl.multiple_of(step * 8, 8)
        for slot, source in enumerate(sources):
            a = source[pl.ds(base, 8)].reshape(8 * B, LANES)
            b = source[pl.ds(base + 16, 8)].reshape(8 * B, LANES)
            both = dot(a, low, ((1,), (0,))) + dot(b, high, ((1,), (0,)))
            out[slot, pl.ds(base, 8)] = both.astype(jnp.bfloat16).reshape(8, B, LANES)
        return carry

    lax.fori_loop(0, 2, body, 0)


M_INVERSE, F_WEIGHT = 0, 1
M_DIAG, M_FACE = 0, 1
C_INVERSE, M_WEIGHT = 0, 1


def row(table, k):
    return table[k : k + 1, :]


def fine_local_kernel(
    f0_hbm, linked_hbm, diag_hbm, faces_hbm, m_inverse_hbm, f_weights_hbm, out, first,
    f0, linked, diag, face, m_inverse, f_weights, semaphores, own,
):
    sources = [f0_hbm, linked_hbm, diag_hbm, faces_hbm.at[0], m_inverse_hbm, f_weights_hbm]
    targets = [f0, linked, diag, face, m_inverse, f_weights]
    copies = [pltpu.make_async_copy(x, y, semaphores.at[k]) for k, (x, y) in enumerate(zip(sources, targets))]
    for copy in copies:
        copy.start()
    for copy in copies[:4]:
        copy.wait()
    own[...] = -f0[...]

    def emit(s, rows, tile):
        out[s, rows, :] = tile

    products([diag, face], [own, linked], B, emit)
    for copy in copies[4:]:
        copy.wait()
    pack_halves([m_inverse, f_weights.at[0], f_weights.at[1]], first)


def chosen(place, index, low, high):
    spot = take_lanes(jnp.broadcast_to(place, (8, LANES)), jnp.broadcast_to(index, (8, LANES)))[0:1]
    inside = (spot >= low) & (spot < high)
    return jnp.clip(spot - low, 0, high - low - 1), inside.astype(jnp.float32)


def gate_of(flow):
    return (flow[0] > 0).astype(jnp.float32)


def fine_flow_kernel(b, known, up, faces, table, flow, out, v):
    index, inside = chosen(up[128:136, :].astype(jnp.int32)[0:1], row(table, F_LINK + 1), 64, 128)
    expand(up[0:128, :].reshape(S, 32, LANES), index, v, inside * gate_of(flow))

    def emit(s, rows, tile):
        out[s, rows, :] = b[s, rows, :] + known[s, rows, :] + tile

    products([faces.at[1]], [v], B, emit)


def fine_down_kernel(
    known, beside, faces, table, first,
    r0, right, f0, sent, longer, v1, v2, wide,
):
    index, inside = chosen(beside[128:136, :].astype(jnp.int32)[0:1], row(table, F_LINK + 2), 64, 128)
    expand(beside[0:128, :].reshape(S, 32, LANES), index, v2, inside)

    def emit_residual(s, rows, tile):
        r0[s, rows, :] = known[s, rows, :] + tile

    products([faces.at[2]], [v2], B, emit_residual)
    residual = r0[...]
    v1[...] = take_lanes(residual, row(table, F_PICK))
    v2[...] = take_lanes(residual, row(table, F_PICK + 1))
    wide[...] = take_lanes(residual, row(table, F_COARSE))
    right[...] = pack(wide[...], 2)

    def emit_right(s, rows, tile):
        right[s, rows, :] += tile

    products([first.at[F_WEIGHT], first.at[F_WEIGHT + 1]], [v1, v2], 32, emit_right)
    expand(right[...], lane_index() % 64, wide)
    mask = (row(table, M_POS) >= 32).astype(jnp.float32)

    def emit_field(s, rows, tile):
        f0[s, rows, :] = tile * mask

    products([first.at[M_INVERSE]], [wide], 32, emit_field)
    expand(f0[...], row(table, M_FINE), wide)
    sent[0:64, :] = pack(wide[...], 4).reshape(64, LANES)
    sent[64:72, :] = table[M_POS:F_POS, :].astype(jnp.float32)
    copy_out(sent, longer)


def middle_local_kernel(
    b, f0, table, m_diag, m_faces, c_inverse, m_weights, out, middle, coarse, own, linked
):
    pack_halves([m_diag, m_faces.at[0], m_faces.at[1], m_faces.at[2]], middle)
    pack_quarters([c_inverse, m_weights.at[0], m_weights.at[1]], coarse)
    expand(-f0[...], lane_index() % 64, own)
    expand(f0[...], row(table, M_LINK), linked)

    def emit(s, rows, tile):
        out[s, rows, :] = b[s, rows, :] + tile

    products([middle.at[M_DIAG], middle.at[M_FACE]], [own, linked], 32, emit)


def middle_flow_kernel(known, up, middle, table, flow, out, v):
    index, inside = chosen(up[64:72, :].astype(jnp.int32)[0:1], row(table, M_LINK + 1), 32, 64)
    expand(up[0:64, :].reshape(S, 16, LANES), index, v, inside * gate_of(flow))

    def emit(s, rows, tile):
        out[s, rows, :] = known[s, rows, :] + tile

    products([middle.at[M_FACE + 1]], [v], 32, emit)


def middle_down_kernel(
    known, beside, middle, coarse, table, flow,
    r0, right, first, longer, v1, v2, wide,
):
    index, inside = chosen(beside[64:72, :].astype(jnp.int32)[0:1], row(table, M_LINK + 2), 32, 64)
    expand(beside[0:64, :].reshape(S, 16, LANES), index, v2, inside)

    def emit_residual(s, rows, tile):
        r0[s, rows, :] = known[s, rows, :] + tile

    products([middle.at[M_FACE + 2]], [v2], 32, emit_residual)
    residual = r0[...]
    expand(residual, row(table, M_PICK), v1)
    expand(residual, row(table, M_PICK + 1), v2)
    expand(residual, row(table, M_COARSE), wide)
    right[...] = pack(wide[...], 4)

    def emit_right(s, rows, tile):
        right[s, rows, :] += tile

    products([coarse.at[M_WEIGHT], coarse.at[M_WEIGHT + 1]], [v1, v2], 16, emit_right)
    expand(right[...], lane_index() % 32, wide)
    start = (flow[0] == 0).astype(jnp.float32)

    def emit_first(s, rows, tile):
        first[s, rows, :] = tile * start

    products([coarse.at[C_INVERSE]], [wide], 16, emit_first)
    copy_field(first, longer)


def coarse_first_kernel(right, own, c_faces, table, out, faces, wide):
    pack_quarters([c_faces.at[0], c_faces.at[1], c_faces.at[2]], faces)
    coarse_local_kernel(right, own, faces, table, out, wide)


def coarse_fine_kernel(right, own, faces, table, f_inverse, f_faces, out, chosen_fine, wide):
    select_fine([f_inverse, f_faces.at[1], f_faces.at[2]], table, chosen_fine)
    coarse_local_kernel(right, own, faces, table, out, wide)


def coarse_middle_kernel(right, own, faces, table, first, middle, out, chosen_middle, wide):
    sources = [first.at[M_INVERSE], middle.at[M_FACE + 1], middle.at[M_FACE + 2]]
    select_middle(sources, table, chosen_middle)
    coarse_local_kernel(right, own, faces, table, out, wide)


def coarse_local_kernel(right, own, faces, table, out, wide):
    expand(own[...], row(table, C_LINK), wide)

    def emit(s, rows, tile):
        out[s, rows, :] = right[s, rows, :] + tile

    products([faces.at[0]], [wide], 16, emit)


def coarse_flow_kernel(known, up, faces, table, flow, out, v):
    expand(up[...], row(table, C_LINK + 1), v, gate_of(flow))

    def emit(s, rows, tile):
        out[s, rows, :] = known[s, rows, :] + tile

    products([faces.at[1]], [v], 16, emit)


def coarse_step_kernel(step, known, own, beside, coarse, faces, table, flow, out, longer, v1, v2, total):
    gate = (step > flow[0]).astype(jnp.float32)
    expand(beside[0:64, :].reshape(S, 16, LANES), row(table, C_LINK + 2), v2, gate)

    def emit_total(s, rows, tile):
        total[s, rows, :] = known[s, rows, :] + tile

    products([faces.at[2]], [v2], 16, emit_total)
    expand(total[...], lane_index() % 32, v1)
    sweep = jnp.broadcast_to(step - flow[0], (8, LANES))

    def emit(s, rows, tile):
        fresh = jnp.where(sweep >= 0, tile, 0.0)
        out[s, rows, :] = jnp.where(sweep < SWEEPS, fresh, own[s, rows, :])

    products([coarse.at[C_INVERSE]], [v1], 16, emit)
    copy_field(out, longer)


def middle_up_local_kernel(r0, f0, fix, up, up_place, middle, chosen_middle, table, flow, out, base, own, linked, known):
    place = row(table, M_POS)
    index, inside = chosen(place, lane_index() % 64, 0, 32)
    expand(fix[...], index, own, inside)
    base[...] = f0[...] + pack(own[...], 2)
    own[...] = -own[...]
    index, inside = chosen(place, row(table, M_LINK), 0, 32)
    expand(fix[...], index, linked, inside)

    def emit(s, rows, tile):
        known[s, rows, :] = r0[s, rows, :] + tile

    products([middle.at[M_DIAG], middle.at[M_FACE]], [own, linked], 32, emit)
    expand(known[...], row(table, M_FINE), own)
    link = pick(row(table, M_LINK + 1), row(table, M_FINE))
    index, inside = chosen(up_place[64:72, :].astype(jnp.int32)[0:1], link, 0, 32)
    expand(up[...], index, linked, inside * gate_of(flow))
    out[...] = pack(own[...], 4)

    def emit_flow(s, rows, tile):
        out[s, rows, :] += tile

    products([chosen_middle.at[1]], [linked], 16, emit_flow)


def middle_up_kernel(known, base, beside, beside_place, chosen_middle, table, out, longer, v1, v2, total, result):
    link = pick(row(table, M_LINK + 2), row(table, M_FINE))
    index, inside = chosen(beside_place[64:72, :].astype(jnp.int32)[0:1], link, 0, 32)
    expand(beside[...], index, v1, inside)

    def emit_total(s, rows, tile):
        total[s, rows, :] = known[s, rows, :] + tile

    products([chosen_middle.at[2]], [v1], 16, emit_total)
    expand(total[...], lane_index() % 32, v2)

    def emit(s, rows, tile):
        result[s, rows, :] = tile

    products([chosen_middle.at[0]], [v2], 16, emit)
    index, inside = chosen(row(table, M_POS), lane_index() % 64, 32, 64)
    expand(result[...], index, v1, inside)
    out[...] = base[...] + pack(v1[...], 2)
    copy_field(out, longer)


def fine_up_local_kernel(r0, f0, fix, diag, faces, table, out, base, own, linked, known):
    place = row(table, F_POS)
    index, inside = chosen(place, lane_index(), 0, 64)
    expand(fix[...], index, own, inside)
    base[...] = f0[...] + own[...]
    own[...] = -own[...]
    index, inside = chosen(place, row(table, F_LINK), 0, 64)
    expand(fix[...], index, linked, inside)

    def emit(s, rows, tile):
        known[s, rows, :] = r0[s, rows, :] + tile

    products([diag, faces.at[0]], [own, linked], B, emit)
    own[...] = take_lanes(known[...], row(table, F_FINE))
    out[...] = pack(own[...], 2)


def fine_up_flow_kernel(known, up, up_place, chosen_fine, table, flow, out, v):
    link = pick(row(table, F_LINK + 1), row(table, F_FINE))
    index, inside = chosen(up_place[128:136, :].astype(jnp.int32)[0:1], link, 0, 64)
    expand(up[...], index, v, inside * gate_of(flow))

    def emit(s, rows, tile):
        out[s, rows, :] = known[s, rows, :] + tile

    products([chosen_fine.at[1]], [v], 32, emit)


def fine_up_kernel(known, base, beside, beside_place, chosen_fine, table, out, v1, v2, total, result):
    link = pick(row(table, F_LINK + 2), row(table, F_FINE))
    index, inside = chosen(beside_place[128:136, :].astype(jnp.int32)[0:1], link, 0, 64)
    expand(beside[0:128, :].reshape(S, 32, LANES), index, v1, inside)

    def emit_total(s, rows, tile):
        total[s, rows, :] = known[s, rows, :] + tile

    products([chosen_fine.at[2]], [v1], 32, emit_total)
    expand(total[...], lane_index() % 64, v2)

    def emit(s, rows, tile):
        result[s, rows, :] = tile

    products([chosen_fine.at[0]], [v2], 32, emit)
    index, inside = chosen(row(table, F_POS), lane_index(), 64, 128)
    expand(result[...], index, v1, inside)
    out[...] = base[...] + v1[...]


WIDE = pltpu.VMEM((S, B, LANES), jnp.float32)


def f32(*shape):
    return jax.ShapeDtypeStruct(shape, jnp.float32)


def bf16(*shape):
    return jax.ShapeDtypeStruct(shape, jnp.bfloat16)


def call(kernel, operands, outs, scratch=(), work=1.0, flow=None, space=pltpu.VMEM, limit=40 * 1024):
    specs = [pl.BlockSpec(memory_space=space)] * len(operands)
    if flow is not None:
        specs.append(pl.BlockSpec(memory_space=pltpu.SMEM))
        operands = (*operands, flow)
    return pl.pallas_call(
        kernel,
        out_shape=outs,
        in_specs=specs,
        out_specs=jax.tree.map(lambda _: pl.BlockSpec(memory_space=pltpu.VMEM), outs),
        scratch_shapes=list(scratch),
        compiler_params=pltpu.CompilerParams(vmem_limit_bytes=limit * 1024),
        cost_estimate=pl.CostEstimate(
            flops=int(work * 4_000_000), bytes_accessed=int(work * 1_000_000), transcendentals=0
        ),
    )(*operands)


def from_behind(block, axis):
    size = lax.axis_size(axis)
    return lax.ppermute(block, axis, [(i, (i + 1) % size) for i in range(size)])


def iterate_from_behind(block, step):
    flow_size, tiles = lax.axis_size("flow"), lax.axis_size("tile")
    route = []
    for g in range(flow_size):
        sends = 0 <= step - 1 - g < SWEEPS - 1
        for t in range(tiles):
            route.append((g * tiles + t, g * tiles + ((t + 1) % tiles if sends else t ^ 1)))
    return lax.ppermute(block, ("flow", "tile"), route)


def own_part(array):
    return array[0, 0]


def shards(*arrays):
    (
        b, f_diag, f_inverse, f_faces, f_links, f_order, f_picks, f_weights,
        m_diag, m_inverse, m_faces, m_links, m_order, m_picks, m_weights,
        c_inverse, c_faces, c_links,
    ) = map(own_part, arrays)
    flow_size = lax.axis_size("flow")
    flow = lax.axis_index("flow").astype(jnp.int32).reshape(1)
    f_order = f_order.reshape(1, LANES)
    m_order = m_order.reshape(1, 64)
    f_links, m_links, c_links = (x.reshape(3, 1, -1) for x in (f_links, m_links, c_links))
    c_inverse, c_faces, m_weights = (jnp.swapaxes(x, -1, -2) for x in (c_inverse, c_faces, m_weights))

    f0, f_linked, f_sent, f_longer, table = call(
        start_kernel,
        (b, f_inverse, f_links, f_order, f_picks, m_links, m_order, m_picks, c_links),
        (
            f32(S, B, LANES), f32(S, B, LANES), f32(136, LANES), f32(136 + SPARE, LANES),
            jax.ShapeDtypeStruct((TABLE, LANES), jnp.int32),
        ),
        (
            WIDE,
            pltpu.VMEM((B, B, LANES), jnp.bfloat16),
            *[pltpu.VMEM(x.shape, jnp.int32) for x in (f_links, f_order, f_picks, m_links, m_order, m_picks, c_links)],
            pltpu.SemaphoreType.DMA((9 + CHUNKS,)),
        ),
        space=pltpu.HBM,
        limit=65000,
    )
    f_beside, f_up = from_behind(f_longer, "tile"), from_behind(f_sent, "flow")
    known, first = call(
        fine_local_kernel,
        (f0, f_linked, f_diag, f_faces, m_inverse, f_weights),
        (f32(S, B, LANES), bf16(3, 32, B, LANES)),
        (
            WIDE,
            WIDE,
            pltpu.VMEM((B, B, LANES), jnp.bfloat16),
            pltpu.VMEM((B, B, LANES), jnp.bfloat16),
            pltpu.VMEM(m_inverse.shape, jnp.bfloat16),
            pltpu.VMEM(f_weights.shape, jnp.bfloat16),
            pltpu.SemaphoreType.DMA((6,)),
            WIDE,
        ),
        3.0,
        space=pltpu.HBM,
        limit=55000,
    )
    known = call(fine_flow_kernel, (b, known, f_up, f_faces, table), f32(S, B, LANES), (WIDE,), 0.0, flow)
    f_r0, right, m_f0, m_sent, m_longer = call(
        fine_down_kernel,
        (known, f_beside, f_faces, table, first),
        (f32(S, B, LANES), f32(S, 32, LANES), f32(S, 32, LANES), f32(72, LANES), f32(72 + SPARE, LANES)),
        (WIDE, WIDE, WIDE),
        2.5,
    )
    m_beside, m_up = from_behind(m_longer, "tile"), from_behind(m_sent, "flow")
    known, middle, coarse = call(
        middle_local_kernel,
        (right, m_f0, table, m_diag, m_faces, c_inverse, m_weights),
        (f32(S, 32, LANES), bf16(4, 32, B, LANES), bf16(3, 16, B, LANES)),
        (WIDE, WIDE),
        2.0,
    )
    known = call(middle_flow_kernel, (known, m_up, middle, table), f32(S, 32, LANES), (WIDE,), 0.0, flow)
    m_r0, right, value, longer = call(
        middle_down_kernel,
        (known, m_beside, middle, coarse, table),
        (f32(S, 32, LANES), f32(S, 16, LANES), f32(S, 16, LANES), f32(64 + SPARE, LANES)),
        (WIDE, WIDE, WIDE),
        1.5,
        flow,
    )
    packed16 = pltpu.VMEM((S, 16, LANES), jnp.float32)
    packed32 = pltpu.VMEM((S, 32, LANES), jnp.float32)
    for step in range(1, SWEEPS + flow_size - 1):
        beside, up = iterate_from_behind(longer, step), from_behind(value, "flow")
        if step == 1:
            known, faces = call(
                coarse_first_kernel,
                (right, value, c_faces, table),
                (f32(S, 16, LANES), bf16(3, 16, B, LANES)),
                (WIDE,),
            )
        elif step == 2:
            known, chosen_fine = call(
                coarse_fine_kernel,
                (right, value, faces, table, f_inverse, f_faces),
                (f32(S, 16, LANES), bf16(3, 32, B, LANES)),
                (WIDE,),
            )
        elif step == 3:
            known, chosen_middle = call(
                coarse_middle_kernel,
                (right, value, faces, table, first, middle),
                (f32(S, 16, LANES), bf16(3, 16, B, LANES)),
                (WIDE,),
            )
        else:
            known = call(coarse_local_kernel, (right, value, faces, table), f32(S, 16, LANES), (WIDE,), 0.25)
        known = call(coarse_flow_kernel, (known, up, faces, table), f32(S, 16, LANES), (WIDE,), 0.0, flow)
        value, longer = call(
            functools.partial(coarse_step_kernel, step),
            (known, value, beside, coarse, faces, table),
            (f32(S, 16, LANES), f32(64 + SPARE, LANES)),
            (WIDE, WIDE, packed16),
            0.5,
            flow,
        )
    beside = from_behind(value, "tile")
    known, base = call(
        middle_up_local_kernel,
        (m_r0, m_f0, value, up, m_up, middle, chosen_middle, table),
        (f32(S, 16, LANES), f32(S, 32, LANES)),
        (WIDE, WIDE, packed32),
        1.25,
        flow,
    )
    fix, longer = call(
        middle_up_kernel,
        (known, base, beside, m_beside, chosen_middle, table),
        (f32(S, 32, LANES), f32(128 + SPARE, LANES)),
        (WIDE, WIDE, packed16, packed16),
        0.5,
    )
    beside, up = from_behind(longer, "tile"), from_behind(fix, "flow")
    known, base = call(
        fine_up_local_kernel,
        (f_r0, f0, fix, f_diag, f_faces, table),
        (f32(S, 32, LANES), f32(S, B, LANES)),
        (WIDE, WIDE, WIDE),
        2.0,
    )
    known = call(fine_up_flow_kernel, (known, up, f_up, chosen_fine, table), f32(S, 32, LANES), (WIDE,), 0.0, flow)
    field = call(
        fine_up_kernel,
        (known, base, beside, f_beside, chosen_fine, table),
        f32(S, B, LANES),
        (WIDE, WIDE, packed32, packed32),
        1.0,
    )
    return field[None, None]


def solution(mesh):
    ranks = (5, 5, 5, 6, 4, 3, 4, 6, 5, 5, 6, 4, 3, 4, 6, 5, 6, 4)
    return jax.shard_map(
        shards,
        mesh=mesh,
        in_specs=tuple(P("flow", "tile", *[None] * (rank - 2)) for rank in ranks),
        out_specs=P("flow", "tile", None, None, None),
        check_vma=False,
    )
```

```python
import functools

import jax
import jax.numpy as jnp
from jax import lax
from jax.experimental import pallas as pl
from jax.experimental.pallas import tpu as pltpu
from jax.sharding import PartitionSpec as P

SWEEPS = 3
S = 4
B = 64
LANES = 128


F_LINK, F_PICK, F_COARSE, F_FINE = 0, 3, 5, 6
M_LINK, M_PICK, M_COARSE, M_FINE = 7, 10, 12, 13
C_LINK, M_POS, F_POS, TABLE = 14, 24, 32, 40


def lane_index():
    return lax.broadcasted_iota(jnp.int32, (1, LANES), 1)


def take_lanes(x, index):
    rows = x.reshape(-1, LANES)
    index = jnp.broadcast_to(index, rows.shape)
    return jnp.take_along_axis(rows, index, axis=1, mode="promise_in_bounds").reshape(x.shape)


def expand(packed, index, out, scale=None):
    rows = packed.shape[1]
    r = B // rows
    for h in range(r):
        values = take_lanes(packed, index + h * (LANES // r))
        if scale is not None:
            values = values * scale
        out[:, h * rows : (h + 1) * rows, :] = values


def pack(wide, r):
    rows = B // r
    group = lane_index() // (LANES // r)
    result = wide[:, :rows, :]
    for h in range(1, r):
        result = jnp.where(group == h, wide[:, h * rows : (h + 1) * rows, :], result)
    return result


def fold(parts):
    row = lax.broadcasted_iota(jnp.int32, (8, LANES), 0)
    high = row >= 4
    mid = (row & 2) > 0
    low = (row & 1) > 0
    level = []
    for i in range(4):
        a, b = parts[i], parts[i + 4]
        level.append(jnp.where(high, b, a) + pltpu.roll(jnp.where(high, a, b), 4, 0))
    pairs = []
    for i in range(2):
        a, b = level[i], level[i + 2]
        pairs.append(jnp.where(mid, b + pltpu.roll(b, 2, 0), a + pltpu.roll(a, 6, 0)))
    a, b = pairs
    return jnp.where(low, b + pltpu.roll(b, 1, 0), a + pltpu.roll(a, 7, 0))


def products(blocks, fields, rows, emit):
    def body(step, carry):
        base = pl.multiple_of(step * 8, 8)
        parts = [[None] * 8 for _ in range(S)]
        for block, field in zip(blocks, fields):
            for i in range(8):
                matrix = block[base + i].astype(jnp.float32)
                for s in range(S):
                    part = jnp.sum((matrix * field[s]).reshape(8, 8, LANES), axis=0)
                    parts[s][i] = part if parts[s][i] is None else parts[s][i] + part
        for s in range(S):
            emit(s, pl.ds(base, 8), fold(parts[s]))
        return carry

    lax.fori_loop(0, rows // 8, body, 0)


def positions(order, n):
    padded = order if n == LANES else jnp.where(lane_index() < n, order, -1)
    hit = padded == lax.broadcasted_iota(jnp.int32, (LANES, LANES), 0)
    place = lax.broadcasted_iota(jnp.int32, (8, LANES), 1).astype(jnp.float32)
    return lax.dot_general(
        place.astype(jnp.bfloat16),
        hit.astype(jnp.float32).astype(jnp.bfloat16),
        (((1,), (1,)), ((), ())),
        preferred_element_type=jnp.float32,
    )


CHUNKS = 4
SPARE = 8


def copy_out(sent, longer):
    rows = sent.shape[0]
    longer[0:rows, :] = sent[...]
    longer[rows : rows + SPARE, :] = jnp.zeros((SPARE, LANES), jnp.float32)


def copy_field(field, longer):
    rows = S * field.shape[1]
    longer[0:rows, :] = field[...].reshape(rows, LANES)
    longer[rows : rows + SPARE, :] = jnp.zeros((SPARE, LANES), jnp.float32)


def spread(values, n):
    return jnp.concatenate([values] * (LANES // n), axis=1)


def pick(source, index):
    source = jnp.broadcast_to(source, (8, LANES))
    return take_lanes(source, jnp.broadcast_to(index, (8, LANES)))[0:1]


def fill_table(f_links, f_order, f_picks, m_links, m_order, m_picks, c_links, table):
    lane = lane_index()

    def put(place, values):
        table[place : place + 1, :] = values

    for k in range(3):
        put(F_LINK + k, f_links[k])
        put(M_LINK + k, spread(m_links[k], 64))
        put(C_LINK + k, spread(c_links[k], 32))
    order = f_order[...]
    wide_order = spread(m_order[...], 64)
    for k in range(2):
        put(F_PICK + k, pick(order, 64 + spread(f_picks[k : k + 1, :], 64)))
        put(M_PICK + k, pick(wide_order, 32 + spread(m_picks[k : k + 1, :], 32)))
    put(F_COARSE, pick(order, lane % 64))
    put(F_FINE, pick(order, 64 + lane % 64))
    put(M_COARSE, pick(wide_order, lane % 32))
    put(M_FINE, pick(wide_order, 32 + lane % 32))
    place = positions(wide_order, 64).astype(jnp.int32)
    table[M_POS:F_POS, :] = take_lanes(place, lane % 64)
    table[F_POS:TABLE, :] = positions(order, LANES).astype(jnp.int32)


def start_kernel(*refs):
    sources, (f0, linked, sent, longer, table) = refs[:9], refs[9:14]
    held, semaphores = refs[14:23], refs[23]
    b, inverse = held[:2]
    rows = B // CHUNKS
    copies = [pltpu.make_async_copy(sources[k], held[k], semaphores.at[k]) for k in (2, 3, 4, 5, 6, 7, 8, 0)]
    parts = []
    for c in range(CHUNKS):
        part = pl.ds(c * rows, rows)
        parts.append(pltpu.make_async_copy(sources[1].at[part], inverse.at[part], semaphores.at[9 + c]))
    for copy in copies + parts:
        copy.start()
    for copy in copies[:7]:
        copy.wait()
    fill_table(*held[2:], table)
    mask = (row(table, F_POS) >= 64).astype(jnp.float32)
    copies[7].wait()
    for c in range(CHUNKS):
        parts[c].wait()

        def emit(s, at, tile):
            f0[s, pl.ds(pl.multiple_of(c * rows + at.start, 8), 8), :] = tile * mask

        products([inverse.at[pl.ds(c * rows, rows)]], [b], rows, emit)
    wide = take_lanes(f0[...], row(table, F_FINE))
    sent[0:128, :] = pack(wide, 2).reshape(128, LANES)
    sent[128:136, :] = table[F_POS:TABLE, :].astype(jnp.float32)
    copy_out(sent, longer)
    linked[...] = take_lanes(f0[...], row(table, F_LINK))


def place_lanes(n, offset):
    shape = (n, LANES)
    source = lax.broadcasted_iota(jnp.int32, shape, 0)
    hit = lax.broadcasted_iota(jnp.int32, shape, 1) == source + offset
    return hit.astype(jnp.float32).astype(jnp.bfloat16)


def dot(a, b, contract):
    return lax.dot_general(a, b, (contract, ((), ())), preferred_element_type=jnp.float32)


def pack_halves(sources, out):
    low, high = place_lanes(64, 0), place_lanes(64, 64)

    def body(step, carry):
        base = pl.multiple_of(step * 8, 8)
        for slot, source in enumerate(sources):
            first = source[pl.ds(base, 8)].reshape(8 * B, 64)
            second = source[pl.ds(base + 32, 8)].reshape(8 * B, 64)
            both = dot(first, low, ((1,), (0,))) + dot(second, high, ((1,), (0,)))
            out[slot, pl.ds(base, 8)] = both.astype(jnp.bfloat16).reshape(8, B, LANES)
        return carry

    lax.fori_loop(0, 4, body, 0)


def pack_quarters(sources, out):
    unit = place_lanes(64, 0)[:, :64]

    def body(step, carry):
        for slot, source in enumerate(sources):
            for k in range(4):
                i = step * 4 + k
                points = jnp.concatenate([source[16 * q + i] for q in range(4)], axis=0)
                out[slot, i] = dot(unit, points, ((1,), (1,))).astype(jnp.bfloat16)
        return carry

    lax.fori_loop(0, 4, body, 0)


def select_fine(sources, table, out):
    source = lax.broadcasted_iota(jnp.int32, (LANES, LANES), 0)
    hit = source == jnp.broadcast_to(row(table, F_FINE), (LANES, LANES))
    first = lax.broadcasted_iota(jnp.int32, (LANES, LANES), 1) < 64
    low = jnp.where(hit & first, 1.0, 0.0).astype(jnp.bfloat16)
    high = jnp.where(hit & ~first, 1.0, 0.0).astype(jnp.bfloat16)

    def body(step, carry):
        base = pl.multiple_of(step * 8, 8)
        for slot, source in enumerate(sources):
            a = source[pl.ds(base, 8)].reshape(8 * B, LANES)
            b = source[pl.ds(base + 32, 8)].reshape(8 * B, LANES)
            both = dot(a, low, ((1,), (0,))) + dot(b, high, ((1,), (0,)))
            out[slot, pl.ds(base, 8)] = both.astype(jnp.bfloat16).reshape(8, B, LANES)
        return carry

    lax.fori_loop(0, 4, body, 0)


def select_middle(sources, table, out):
    source = lax.broadcasted_iota(jnp.int32, (LANES, LANES), 0)
    group = lax.broadcasted_iota(jnp.int32, (LANES, LANES), 1) // 32
    hit = source == jnp.broadcast_to(row(table, M_FINE), (LANES, LANES)) + 64 * (group // 2)
    low = jnp.where(hit & (group % 2 == 0), 1.0, 0.0).astype(jnp.bfloat16)
    high = jnp.where(hit & (group % 2 == 1), 1.0, 0.0).astype(jnp.bfloat16)

    def body(step, carry):
        base = pl.multiple_of(step * 8, 8)
        for slot, source in enumerate(sources):
            a = source[pl.ds(base, 8)].reshape(8 * B, LANES)
            b = source[pl.ds(base + 16, 8)].reshape(8 * B, LANES)
            both = dot(a, low, ((1,), (0,))) + dot(b, high, ((1,), (0,)))
            out[slot, pl.ds(base, 8)] = both.astype(jnp.bfloat16).reshape(8, B, LANES)
        return carry

    lax.fori_loop(0, 2, body, 0)


M_INVERSE, F_WEIGHT = 0, 1
M_DIAG, M_FACE = 0, 1
C_INVERSE, M_WEIGHT = 0, 1


def row(table, k):
    return table[k : k + 1, :]


def fine_local_kernel(
    f0_hbm, linked_hbm, diag_hbm, faces_hbm, m_inverse_hbm, f_weights_hbm, out, first_hbm,
    f0, linked, diag, face, m_inverse, f_weights, first, semaphores, own,
):
    sources = [m_inverse_hbm, f_weights_hbm, f0_hbm, linked_hbm, diag_hbm, faces_hbm.at[0]]
    targets = [m_inverse, f_weights, f0, linked, diag, face]
    copies = [pltpu.make_async_copy(x, y, semaphores.at[k]) for k, (x, y) in enumerate(zip(sources, targets))]
    for copy in copies:
        copy.start()
    for copy in copies[:2]:
        copy.wait()
    pack_halves([m_inverse, f_weights.at[0], f_weights.at[1]], first)
    packed = pltpu.make_async_copy(first, first_hbm, semaphores.at[6])
    packed.start()
    for copy in copies[2:]:
        copy.wait()
    own[...] = -f0[...]

    def emit(s, rows, tile):
        out[s, rows, :] = tile

    products([diag, face], [own, linked], B, emit)
    packed.wait()


def chosen(place, index, low, high):
    spot = take_lanes(jnp.broadcast_to(place, (8, LANES)), jnp.broadcast_to(index, (8, LANES)))[0:1]
    inside = (spot >= low) & (spot < high)
    return jnp.clip(spot - low, 0, high - low - 1), inside.astype(jnp.float32)


def gate_of(flow):
    return (flow[0] > 0).astype(jnp.float32)


def fine_flow_kernel(b, known, up, faces, table, flow, out, v):
    index, inside = chosen(up[128:136, :].astype(jnp.int32)[0:1], row(table, F_LINK + 1), 64, 128)
    expand(up[0:128, :].reshape(S, 32, LANES), index, v, inside * gate_of(flow))

    def emit(s, rows, tile):
        out[s, rows, :] = b[s, rows, :] + known[s, rows, :] + tile

    products([faces.at[1]], [v], B, emit)


def fine_down_kernel(
    known, beside, faces, table, first,
    r0, right, f0, sent, longer, v1, v2, wide,
):
    index, inside = chosen(beside[128:136, :].astype(jnp.int32)[0:1], row(table, F_LINK + 2), 64, 128)
    expand(beside[0:128, :].reshape(S, 32, LANES), index, v2, inside)

    def emit_residual(s, rows, tile):
        r0[s, rows, :] = known[s, rows, :] + tile

    products([faces.at[2]], [v2], B, emit_residual)
    residual = r0[...]
    v1[...] = take_lanes(residual, row(table, F_PICK))
    v2[...] = take_lanes(residual, row(table, F_PICK + 1))
    wide[...] = take_lanes(residual, row(table, F_COARSE))
    right[...] = pack(wide[...], 2)

    def emit_right(s, rows, tile):
        right[s, rows, :] += tile

    products([first.at[F_WEIGHT], first.at[F_WEIGHT + 1]], [v1, v2], 32, emit_right)
    expand(right[...], lane_index() % 64, wide)
    mask = (row(table, M_POS) >= 32).astype(jnp.float32)

    def emit_field(s, rows, tile):
        f0[s, rows, :] = tile * mask

    products([first.at[M_INVERSE]], [wide], 32, emit_field)
    expand(f0[...], row(table, M_FINE), wide)
    sent[0:64, :] = pack(wide[...], 4).reshape(64, LANES)
    sent[64:72, :] = table[M_POS:F_POS, :].astype(jnp.float32)
    copy_out(sent, longer)


def middle_local_kernel(
    b, f0, table, m_diag, m_faces, c_inverse, m_weights, out, middle, coarse, own, linked
):
    pack_halves([m_diag, m_faces.at[0], m_faces.at[1], m_faces.at[2]], middle)
    pack_quarters([c_inverse, m_weights.at[0], m_weights.at[1]], coarse)
    expand(-f0[...], lane_index() % 64, own)
    expand(f0[...], row(table, M_LINK), linked)

    def emit(s, rows, tile):
        out[s, rows, :] = b[s, rows, :] + tile

    products([middle.at[M_DIAG], middle.at[M_FACE]], [own, linked], 32, emit)


def middle_flow_kernel(known, up, middle, table, flow, out, v):
    index, inside = chosen(up[64:72, :].astype(jnp.int32)[0:1], row(table, M_LINK + 1), 32, 64)
    expand(up[0:64, :].reshape(S, 16, LANES), index, v, inside * gate_of(flow))

    def emit(s, rows, tile):
        out[s, rows, :] = known[s, rows, :] + tile

    products([middle.at[M_FACE + 1]], [v], 32, emit)


def middle_down_kernel(
    known, beside, middle, coarse, table, flow,
    r0, right, first, longer, v1, v2, wide,
):
    index, inside = chosen(beside[64:72, :].astype(jnp.int32)[0:1], row(table, M_LINK + 2), 32, 64)
    expand(beside[0:64, :].reshape(S, 16, LANES), index, v2, inside)

    def emit_residual(s, rows, tile):
        r0[s, rows, :] = known[s, rows, :] + tile

    products([middle.at[M_FACE + 2]], [v2], 32, emit_residual)
    residual = r0[...]
    expand(residual, row(table, M_PICK), v1)
    expand(residual, row(table, M_PICK + 1), v2)
    expand(residual, row(table, M_COARSE), wide)
    right[...] = pack(wide[...], 4)

    def emit_right(s, rows, tile):
        right[s, rows, :] += tile

    products([coarse.at[M_WEIGHT], coarse.at[M_WEIGHT + 1]], [v1, v2], 16, emit_right)
    expand(right[...], lane_index() % 32, wide)
    start = (flow[0] == 0).astype(jnp.float32)

    def emit_first(s, rows, tile):
        first[s, rows, :] = tile * start

    products([coarse.at[C_INVERSE]], [wide], 16, emit_first)
    copy_field(first, longer)


def coarse_first_kernel(right, own, c_faces, table, out, faces, wide):
    pack_quarters([c_faces.at[0], c_faces.at[1], c_faces.at[2]], faces)
    coarse_local_kernel(right, own, faces, table, out, wide)


def coarse_fine_kernel(right, own, faces, table, f_inverse, f_faces, out, chosen_fine, wide):
    select_fine([f_inverse, f_faces.at[1], f_faces.at[2]], table, chosen_fine)
    coarse_local_kernel(right, own, faces, table, out, wide)


def coarse_middle_kernel(right, own, faces, table, first, middle, out, chosen_middle, wide):
    sources = [first.at[M_INVERSE], middle.at[M_FACE + 1], middle.at[M_FACE + 2]]
    select_middle(sources, table, chosen_middle)
    coarse_local_kernel(right, own, faces, table, out, wide)


def coarse_local_kernel(right, own, faces, table, out, wide):
    expand(own[...], row(table, C_LINK), wide)

    def emit(s, rows, tile):
        out[s, rows, :] = right[s, rows, :] + tile

    products([faces.at[0]], [wide], 16, emit)


def coarse_flow_kernel(known, up, faces, table, flow, out, v):
    expand(up[...], row(table, C_LINK + 1), v, gate_of(flow))

    def emit(s, rows, tile):
        out[s, rows, :] = known[s, rows, :] + tile

    products([faces.at[1]], [v], 16, emit)


def coarse_step_kernel(step, known, own, beside, coarse, faces, table, flow, out, longer, v1, v2, total):
    gate = (step > flow[0]).astype(jnp.float32)
    expand(beside[0:64, :].reshape(S, 16, LANES), row(table, C_LINK + 2), v2, gate)

    def emit_total(s, rows, tile):
        total[s, rows, :] = known[s, rows, :] + tile

    products([faces.at[2]], [v2], 16, emit_total)
    expand(total[...], lane_index() % 32, v1)
    sweep = jnp.broadcast_to(step - flow[0], (8, LANES))

    def emit(s, rows, tile):
        fresh = jnp.where(sweep >= 0, tile, 0.0)
        out[s, rows, :] = jnp.where(sweep < SWEEPS, fresh, own[s, rows, :])

    products([coarse.at[C_INVERSE]], [v1], 16, emit)
    copy_field(out, longer)


def middle_up_local_kernel(r0, f0, fix, up, up_place, middle, chosen_middle, table, flow, out, base, own, linked, known):
    place = row(table, M_POS)
    index, inside = chosen(place, lane_index() % 64, 0, 32)
    expand(fix[...], index, own, inside)
    base[...] = f0[...] + pack(own[...], 2)
    own[...] = -own[...]
    index, inside = chosen(place, row(table, M_LINK), 0, 32)
    expand(fix[...], index, linked, inside)

    def emit(s, rows, tile):
        known[s, rows, :] = r0[s, rows, :] + tile

    products([middle.at[M_DIAG], middle.at[M_FACE]], [own, linked], 32, emit)
    expand(known[...], row(table, M_FINE), own)
    link = pick(row(table, M_LINK + 1), row(table, M_FINE))
    index, inside = chosen(up_place[64:72, :].astype(jnp.int32)[0:1], link, 0, 32)
    expand(up[...], index, linked, inside * gate_of(flow))
    out[...] = pack(own[...], 4)

    def emit_flow(s, rows, tile):
        out[s, rows, :] += tile

    products([chosen_middle.at[1]], [linked], 16, emit_flow)


def middle_up_kernel(known, base, beside, beside_place, chosen_middle, table, out, longer, v1, v2, total, result):
    link = pick(row(table, M_LINK + 2), row(table, M_FINE))
    index, inside = chosen(beside_place[64:72, :].astype(jnp.int32)[0:1], link, 0, 32)
    expand(beside[0:64, :].reshape(S, 16, LANES), index, v1, inside)

    def emit_total(s, rows, tile):
        total[s, rows, :] = known[s, rows, :] + tile

    products([chosen_middle.at[2]], [v1], 16, emit_total)
    expand(total[...], lane_index() % 32, v2)

    def emit(s, rows, tile):
        result[s, rows, :] = tile

    products([chosen_middle.at[0]], [v2], 16, emit)
    index, inside = chosen(row(table, M_POS), lane_index() % 64, 32, 64)
    expand(result[...], index, v1, inside)
    out[...] = base[...] + pack(v1[...], 2)
    copy_field(out, longer)


def fine_up_local_kernel(r0, f0, fix, diag, faces, table, out, base, own, linked, known):
    place = row(table, F_POS)
    index, inside = chosen(place, lane_index(), 0, 64)
    expand(fix[...], index, own, inside)
    base[...] = f0[...] + own[...]
    own[...] = -own[...]
    index, inside = chosen(place, row(table, F_LINK), 0, 64)
    expand(fix[...], index, linked, inside)

    def emit(s, rows, tile):
        known[s, rows, :] = r0[s, rows, :] + tile

    products([diag, faces.at[0]], [own, linked], B, emit)
    own[...] = take_lanes(known[...], row(table, F_FINE))
    out[...] = pack(own[...], 2)


def fine_up_flow_kernel(known, up, up_place, chosen_fine, table, flow, out, v):
    link = pick(row(table, F_LINK + 1), row(table, F_FINE))
    index, inside = chosen(up_place[128:136, :].astype(jnp.int32)[0:1], link, 0, 64)
    expand(up[...], index, v, inside * gate_of(flow))

    def emit(s, rows, tile):
        out[s, rows, :] = known[s, rows, :] + tile

    products([chosen_fine.at[1]], [v], 32, emit)


def fine_up_kernel(known, base, beside, beside_place, chosen_fine, table, out, v1, v2, total, result):
    link = pick(row(table, F_LINK + 2), row(table, F_FINE))
    index, inside = chosen(beside_place[128:136, :].astype(jnp.int32)[0:1], link, 0, 64)
    expand(beside[0:128, :].reshape(S, 32, LANES), index, v1, inside)

    def emit_total(s, rows, tile):
        total[s, rows, :] = known[s, rows, :] + tile

    products([chosen_fine.at[2]], [v1], 32, emit_total)
    expand(total[...], lane_index() % 64, v2)

    def emit(s, rows, tile):
        result[s, rows, :] = tile

    products([chosen_fine.at[0]], [v2], 32, emit)
    index, inside = chosen(row(table, F_POS), lane_index(), 64, 128)
    expand(result[...], index, v1, inside)
    out[...] = base[...] + v1[...]


WIDE = pltpu.VMEM((S, B, LANES), jnp.float32)


def f32(*shape):
    return jax.ShapeDtypeStruct(shape, jnp.float32)


def bf16(*shape):
    return jax.ShapeDtypeStruct(shape, jnp.bfloat16)


def call(kernel, operands, outs, scratch=(), work=1.0, flow=None, space=pltpu.VMEM, limit=40 * 1024, out_spaces=None):
    specs = [pl.BlockSpec(memory_space=space)] * len(operands)
    if flow is not None:
        specs.append(pl.BlockSpec(memory_space=pltpu.SMEM))
        operands = (*operands, flow)
    return pl.pallas_call(
        kernel,
        out_shape=outs,
        in_specs=specs,
        out_specs=jax.tree.map(lambda _: pl.BlockSpec(memory_space=pltpu.VMEM), outs)
        if out_spaces is None
        else tuple(pl.BlockSpec(memory_space=x) for x in out_spaces),
        scratch_shapes=list(scratch),
        compiler_params=pltpu.CompilerParams(vmem_limit_bytes=limit * 1024),
        cost_estimate=pl.CostEstimate(
            flops=int(work * 4_000_000), bytes_accessed=int(work * 1_000_000), transcendentals=0
        ),
    )(*operands)


def from_behind(block, axis):
    size = lax.axis_size(axis)
    return lax.ppermute(block, axis, [(i, (i + 1) % size) for i in range(size)])


def iterate_from_behind(block, step):
    flow_size, tiles = lax.axis_size("flow"), lax.axis_size("tile")
    route = []
    for g in range(flow_size):
        sends = 0 <= step - 1 - g < SWEEPS - 1
        for t in range(tiles):
            route.append((g * tiles + t, g * tiles + ((t + 1) % tiles if sends else t ^ 1)))
    return lax.ppermute(block, ("flow", "tile"), route)


def own_part(array):
    return array[0, 0]


def shards(*arrays):
    (
        b, f_diag, f_inverse, f_faces, f_links, f_order, f_picks, f_weights,
        m_diag, m_inverse, m_faces, m_links, m_order, m_picks, m_weights,
        c_inverse, c_faces, c_links,
    ) = map(own_part, arrays)
    flow_size = lax.axis_size("flow")
    flow = lax.axis_index("flow").astype(jnp.int32).reshape(1)
    f_order = f_order.reshape(1, LANES)
    m_order = m_order.reshape(1, 64)
    f_links, m_links, c_links = (x.reshape(3, 1, -1) for x in (f_links, m_links, c_links))
    c_inverse, c_faces, m_weights = (jnp.swapaxes(x, -1, -2) for x in (c_inverse, c_faces, m_weights))

    f0, f_linked, f_sent, f_longer, table = call(
        start_kernel,
        (b, f_inverse, f_links, f_order, f_picks, m_links, m_order, m_picks, c_links),
        (
            f32(S, B, LANES), f32(S, B, LANES), f32(136, LANES), f32(136 + SPARE, LANES),
            jax.ShapeDtypeStruct((TABLE, LANES), jnp.int32),
        ),
        (
            WIDE,
            pltpu.VMEM((B, B, LANES), jnp.bfloat16),
            *[pltpu.VMEM(x.shape, jnp.int32) for x in (f_links, f_order, f_picks, m_links, m_order, m_picks, c_links)],
            pltpu.SemaphoreType.DMA((9 + CHUNKS,)),
        ),
        space=pltpu.HBM,
        limit=65000,
    )
    f_beside, f_up = from_behind(f_longer, "tile"), from_behind(f_sent, "flow")
    known, first = call(
        fine_local_kernel,
        (f0, f_linked, f_diag, f_faces, m_inverse, f_weights),
        (f32(S, B, LANES), bf16(3, 32, B, LANES)),
        (
            WIDE,
            WIDE,
            pltpu.VMEM((B, B, LANES), jnp.bfloat16),
            pltpu.VMEM((B, B, LANES), jnp.bfloat16),
            pltpu.VMEM(m_inverse.shape, jnp.bfloat16),
            pltpu.VMEM(f_weights.shape, jnp.bfloat16),
            pltpu.VMEM((3, 32, B, LANES), jnp.bfloat16),
            pltpu.SemaphoreType.DMA((7,)),
            WIDE,
        ),
        3.0,
        space=pltpu.HBM,
        limit=55000,
        out_spaces=(pltpu.VMEM, pltpu.HBM),
    )
    known = call(fine_flow_kernel, (b, known, f_up, f_faces, table), f32(S, B, LANES), (WIDE,), 0.0, flow)
    f_r0, right, m_f0, m_sent, m_longer = call(
        fine_down_kernel,
        (known, f_beside, f_faces, table, first),
        (f32(S, B, LANES), f32(S, 32, LANES), f32(S, 32, LANES), f32(72, LANES), f32(72 + SPARE, LANES)),
        (WIDE, WIDE, WIDE),
        2.5,
    )
    m_beside, m_up = from_behind(m_longer, "tile"), from_behind(m_sent, "flow")
    known, middle, coarse = call(
        middle_local_kernel,
        (right, m_f0, table, m_diag, m_faces, c_inverse, m_weights),
        (f32(S, 32, LANES), bf16(4, 32, B, LANES), bf16(3, 16, B, LANES)),
        (WIDE, WIDE),
        2.0,
    )
    known = call(middle_flow_kernel, (known, m_up, middle, table), f32(S, 32, LANES), (WIDE,), 0.0, flow)
    m_r0, right, value, longer = call(
        middle_down_kernel,
        (known, m_beside, middle, coarse, table),
        (f32(S, 32, LANES), f32(S, 16, LANES), f32(S, 16, LANES), f32(64 + SPARE, LANES)),
        (WIDE, WIDE, WIDE),
        1.5,
        flow,
    )
    packed16 = pltpu.VMEM((S, 16, LANES), jnp.float32)
    packed32 = pltpu.VMEM((S, 32, LANES), jnp.float32)
    for step in range(1, SWEEPS + flow_size - 1):
        beside, up = iterate_from_behind(longer, step), from_behind(value, "flow")
        if step == 1:
            known, faces = call(
                coarse_first_kernel,
                (right, value, c_faces, table),
                (f32(S, 16, LANES), bf16(3, 16, B, LANES)),
                (WIDE,),
            )
        elif step == 2:
            known, chosen_fine = call(
                coarse_fine_kernel,
                (right, value, faces, table, f_inverse, f_faces),
                (f32(S, 16, LANES), bf16(3, 32, B, LANES)),
                (WIDE,),
            )
        elif step == 3:
            known, chosen_middle = call(
                coarse_middle_kernel,
                (right, value, faces, table, first, middle),
                (f32(S, 16, LANES), bf16(3, 16, B, LANES)),
                (WIDE,),
            )
        else:
            known = call(coarse_local_kernel, (right, value, faces, table), f32(S, 16, LANES), (WIDE,), 0.25)
        known = call(coarse_flow_kernel, (known, up, faces, table), f32(S, 16, LANES), (WIDE,), 0.0, flow)
        value, longer = call(
            functools.partial(coarse_step_kernel, step),
            (known, value, beside, coarse, faces, table),
            (f32(S, 16, LANES), f32(64 + SPARE, LANES)),
            (WIDE, WIDE, packed16),
            0.5,
            flow,
        )
    beside = from_behind(longer, "tile")
    known, base = call(
        middle_up_local_kernel,
        (m_r0, m_f0, value, up, m_up, middle, chosen_middle, table),
        (f32(S, 16, LANES), f32(S, 32, LANES)),
        (WIDE, WIDE, packed32),
        1.25,
        flow,
    )
    fix, longer = call(
        middle_up_kernel,
        (known, base, beside, m_beside, chosen_middle, table),
        (f32(S, 32, LANES), f32(128 + SPARE, LANES)),
        (WIDE, WIDE, packed16, packed16),
        0.5,
    )
    beside, up = from_behind(longer, "tile"), from_behind(fix, "flow")
    known, base = call(
        fine_up_local_kernel,
        (f_r0, f0, fix, f_diag, f_faces, table),
        (f32(S, 32, LANES), f32(S, B, LANES)),
        (WIDE, WIDE, WIDE),
        2.0,
    )
    known = call(fine_up_flow_kernel, (known, up, f_up, chosen_fine, table), f32(S, 32, LANES), (WIDE,), 0.0, flow)
    field = call(
        fine_up_kernel,
        (known, base, beside, f_beside, chosen_fine, table),
        f32(S, B, LANES),
        (WIDE, WIDE, packed32, packed32),
        1.0,
    )
    return field[None, None]


def solution(mesh):
    ranks = (5, 5, 5, 6, 4, 3, 4, 6, 5, 5, 6, 4, 3, 4, 6, 5, 6, 4)
    return jax.shard_map(
        shards,
        mesh=mesh,
        in_specs=tuple(P("flow", "tile", *[None] * (rank - 2)) for rank in ranks),
        out_specs=P("flow", "tile", None, None, None),
        check_vma=False,
    )
```

```python
import functools

import jax
import jax.numpy as jnp
from jax import lax
from jax.experimental import pallas as pl
from jax.experimental.pallas import tpu as pltpu
from jax.sharding import PartitionSpec as P

SWEEPS = 3
S = 4
B = 64
LANES = 128


F_LINK, F_PICK, F_COARSE, F_FINE = 0, 3, 5, 6
M_LINK, M_PICK, M_COARSE, M_FINE = 7, 10, 12, 13
C_LINK, M_POS, F_POS, TABLE = 14, 24, 32, 40


def lane_index():
    return lax.broadcasted_iota(jnp.int32, (1, LANES), 1)


def take_lanes(x, index):
    rows = x.reshape(-1, LANES)
    index = jnp.broadcast_to(index, rows.shape)
    return jnp.take_along_axis(rows, index, axis=1, mode="promise_in_bounds").reshape(x.shape)


def expand(packed, index, out, scale=None):
    rows = packed.shape[1]
    r = B // rows
    for h in range(r):
        values = take_lanes(packed, index + h * (LANES // r))
        if scale is not None:
            values = values * scale
        out[:, h * rows : (h + 1) * rows, :] = values


def pack(wide, r):
    rows = B // r
    group = lane_index() // (LANES // r)
    result = wide[:, :rows, :]
    for h in range(1, r):
        result = jnp.where(group == h, wide[:, h * rows : (h + 1) * rows, :], result)
    return result


def fold(parts):
    row = lax.broadcasted_iota(jnp.int32, (8, LANES), 0)
    high = row >= 4
    mid = (row & 2) > 0
    low = (row & 1) > 0
    level = []
    for i in range(4):
        a, b = parts[i], parts[i + 4]
        level.append(jnp.where(high, b, a) + pltpu.roll(jnp.where(high, a, b), 4, 0))
    pairs = []
    for i in range(2):
        a, b = level[i], level[i + 2]
        pairs.append(jnp.where(mid, b + pltpu.roll(b, 2, 0), a + pltpu.roll(a, 6, 0)))
    a, b = pairs
    return jnp.where(low, b + pltpu.roll(b, 1, 0), a + pltpu.roll(a, 7, 0))


def products(blocks, fields, rows, emit):
    def body(step, carry):
        base = pl.multiple_of(step * 8, 8)
        parts = [[None] * 8 for _ in range(S)]
        for block, field in zip(blocks, fields):
            for i in range(8):
                matrix = block[base + i].astype(jnp.float32)
                for s in range(S):
                    part = jnp.sum((matrix * field[s]).reshape(8, 8, LANES), axis=0)
                    parts[s][i] = part if parts[s][i] is None else parts[s][i] + part
        for s in range(S):
            emit(s, pl.ds(base, 8), fold(parts[s]))
        return carry

    lax.fori_loop(0, rows // 8, body, 0)


def positions(order, n):
    padded = order if n == LANES else jnp.where(lane_index() < n, order, -1)
    hit = padded == lax.broadcasted_iota(jnp.int32, (LANES, LANES), 0)
    place = lax.broadcasted_iota(jnp.int32, (8, LANES), 1).astype(jnp.float32)
    return lax.dot_general(
        place.astype(jnp.bfloat16),
        hit.astype(jnp.float32).astype(jnp.bfloat16),
        (((1,), (1,)), ((), ())),
        preferred_element_type=jnp.float32,
    )


CHUNKS = 4
SPARE = 8


def copy_out(sent, longer):
    rows = sent.shape[0]
    longer[0:rows, :] = sent[...]
    longer[rows : rows + SPARE, :] = jnp.zeros((SPARE, LANES), jnp.float32)


def copy_field(field, longer):
    rows = S * field.shape[1]
    longer[0:rows, :] = field[...].reshape(rows, LANES)
    longer[rows : rows + SPARE, :] = jnp.zeros((SPARE, LANES), jnp.float32)


def spread(values, n):
    return jnp.concatenate([values] * (LANES // n), axis=1)


def pick(source, index):
    source = jnp.broadcast_to(source, (8, LANES))
    return take_lanes(source, jnp.broadcast_to(index, (8, LANES)))[0:1]


def fill_table(f_links, f_order, f_picks, m_links, m_order, m_picks, c_links, table):
    lane = lane_index()

    def put(place, values):
        table[place : place + 1, :] = values

    for k in range(3):
        put(F_LINK + k, f_links[k])
        put(M_LINK + k, spread(m_links[k], 64))
        put(C_LINK + k, spread(c_links[k], 32))
    order = f_order[...]
    wide_order = spread(m_order[...], 64)
    for k in range(2):
        put(F_PICK + k, pick(order, 64 + spread(f_picks[k : k + 1, :], 64)))
        put(M_PICK + k, pick(wide_order, 32 + spread(m_picks[k : k + 1, :], 32)))
    put(F_COARSE, pick(order, lane % 64))
    put(F_FINE, pick(order, 64 + lane % 64))
    put(M_COARSE, pick(wide_order, lane % 32))
    put(M_FINE, pick(wide_order, 32 + lane % 32))
    place = positions(wide_order, 64).astype(jnp.int32)
    table[M_POS:F_POS, :] = take_lanes(place, lane % 64)
    table[F_POS:TABLE, :] = positions(order, LANES).astype(jnp.int32)


def start_kernel(*refs):
    sources, (f0, linked, sent, longer, table) = refs[:9], refs[9:14]
    held, semaphores = refs[14:23], refs[23]
    b, inverse = held[:2]
    rows = B // CHUNKS
    copies = [pltpu.make_async_copy(sources[k], held[k], semaphores.at[k]) for k in (2, 3, 4, 5, 6, 7, 8, 0)]
    parts = []
    for c in range(CHUNKS):
        part = pl.ds(c * rows, rows)
        parts.append(pltpu.make_async_copy(sources[1].at[part], inverse.at[part], semaphores.at[9 + c]))
    for copy in copies + parts:
        copy.start()
    for copy in copies[:7]:
        copy.wait()
    fill_table(*held[2:], table)
    mask = (row(table, F_POS) >= 64).astype(jnp.float32)
    copies[7].wait()
    for c in range(CHUNKS):
        parts[c].wait()

        def emit(s, at, tile):
            f0[s, pl.ds(pl.multiple_of(c * rows + at.start, 8), 8), :] = tile * mask

        products([inverse.at[pl.ds(c * rows, rows)]], [b], rows, emit)
    wide = take_lanes(f0[...], row(table, F_FINE))
    sent[0:128, :] = pack(wide, 2).reshape(128, LANES)
    sent[128:136, :] = table[F_POS:TABLE, :].astype(jnp.float32)
    copy_out(sent, longer)
    linked[...] = take_lanes(f0[...], row(table, F_LINK))


def place_lanes(n, offset):
    shape = (n, LANES)
    source = lax.broadcasted_iota(jnp.int32, shape, 0)
    hit = lax.broadcasted_iota(jnp.int32, shape, 1) == source + offset
    return hit.astype(jnp.float32).astype(jnp.bfloat16)


def dot(a, b, contract):
    return lax.dot_general(a, b, (contract, ((), ())), preferred_element_type=jnp.float32)


def pack_halves(sources, out):
    low, high = place_lanes(64, 0), place_lanes(64, 64)

    def body(step, carry):
        base = pl.multiple_of(step * 8, 8)
        for slot, source in enumerate(sources):
            first = source[pl.ds(base, 8)].reshape(8 * B, 64)
            second = source[pl.ds(base + 32, 8)].reshape(8 * B, 64)
            both = dot(first, low, ((1,), (0,))) + dot(second, high, ((1,), (0,)))
            out[slot, pl.ds(base, 8)] = both.astype(jnp.bfloat16).reshape(8, B, LANES)
        return carry

    lax.fori_loop(0, 4, body, 0)


def pack_quarters(sources, out):
    unit = place_lanes(64, 0)[:, :64]

    def body(step, carry):
        for slot, source in enumerate(sources):
            for k in range(4):
                i = step * 4 + k
                points = jnp.concatenate([source[16 * q + i] for q in range(4)], axis=0)
                out[slot, i] = dot(unit, points, ((1,), (1,))).astype(jnp.bfloat16)
        return carry

    lax.fori_loop(0, 4, body, 0)


def select_fine(sources, table, out):
    source = lax.broadcasted_iota(jnp.int32, (LANES, LANES), 0)
    hit = source == jnp.broadcast_to(row(table, F_FINE), (LANES, LANES))
    first = lax.broadcasted_iota(jnp.int32, (LANES, LANES), 1) < 64
    low = jnp.where(hit & first, 1.0, 0.0).astype(jnp.bfloat16)
    high = jnp.where(hit & ~first, 1.0, 0.0).astype(jnp.bfloat16)

    def body(step, carry):
        base = pl.multiple_of(step * 8, 8)
        for slot, source in enumerate(sources):
            a = source[pl.ds(base, 8)].reshape(8 * B, LANES)
            b = source[pl.ds(base + 32, 8)].reshape(8 * B, LANES)
            both = dot(a, low, ((1,), (0,))) + dot(b, high, ((1,), (0,)))
            out[slot, pl.ds(base, 8)] = both.astype(jnp.bfloat16).reshape(8, B, LANES)
        return carry

    lax.fori_loop(0, 4, body, 0)


def select_middle(sources, table, out):
    source = lax.broadcasted_iota(jnp.int32, (LANES, LANES), 0)
    group = lax.broadcasted_iota(jnp.int32, (LANES, LANES), 1) // 32
    hit = source == jnp.broadcast_to(row(table, M_FINE), (LANES, LANES)) + 64 * (group // 2)
    low = jnp.where(hit & (group % 2 == 0), 1.0, 0.0).astype(jnp.bfloat16)
    high = jnp.where(hit & (group % 2 == 1), 1.0, 0.0).astype(jnp.bfloat16)

    def body(step, carry):
        base = pl.multiple_of(step * 8, 8)
        for slot, source in enumerate(sources):
            a = source[pl.ds(base, 8)].reshape(8 * B, LANES)
            b = source[pl.ds(base + 16, 8)].reshape(8 * B, LANES)
            both = dot(a, low, ((1,), (0,))) + dot(b, high, ((1,), (0,)))
            out[slot, pl.ds(base, 8)] = both.astype(jnp.bfloat16).reshape(8, B, LANES)
        return carry

    lax.fori_loop(0, 2, body, 0)


M_INVERSE, F_WEIGHT, M_NEXT = 0, 1, 3
M_DIAG, M_FACE = 0, 1
C_INVERSE, M_WEIGHT = 0, 1


def row(table, k):
    return table[k : k + 1, :]


def fine_local_kernel(
    f0_hbm, linked_hbm, diag_hbm, faces_hbm, m_inverse_hbm, f_weights_hbm, m_faces_hbm, out, first_hbm,
    f0, linked, diag, face, m_inverse, f_weights, m_faces, first, semaphores, own,
):
    sources = [m_inverse_hbm, f_weights_hbm, m_faces_hbm.at[pl.ds(1, 2)], f0_hbm, linked_hbm, diag_hbm, faces_hbm.at[0]]
    targets = [m_inverse, f_weights, m_faces, f0, linked, diag, face]
    copies = [pltpu.make_async_copy(x, y, semaphores.at[k]) for k, (x, y) in enumerate(zip(sources, targets))]
    for copy in copies:
        copy.start()
    for copy in copies[:3]:
        copy.wait()
    pack_halves([m_inverse, f_weights.at[0], f_weights.at[1], m_faces.at[0], m_faces.at[1]], first)
    packed = pltpu.make_async_copy(first, first_hbm, semaphores.at[7])
    packed.start()
    for copy in copies[3:]:
        copy.wait()
    own[...] = -f0[...]

    def emit(s, rows, tile):
        out[s, rows, :] = tile

    products([diag, face], [own, linked], B, emit)
    packed.wait()


def chosen(place, index, low, high):
    spot = take_lanes(jnp.broadcast_to(place, (8, LANES)), jnp.broadcast_to(index, (8, LANES)))[0:1]
    inside = (spot >= low) & (spot < high)
    return jnp.clip(spot - low, 0, high - low - 1), inside.astype(jnp.float32)


def gate_of(flow):
    return (flow[0] > 0).astype(jnp.float32)


def fine_flow_kernel(b, known, up, faces, table, flow, out, v):
    index, inside = chosen(up[128:136, :].astype(jnp.int32)[0:1], row(table, F_LINK + 1), 64, 128)
    expand(up[0:128, :].reshape(S, 32, LANES), index, v, inside * gate_of(flow))

    def emit(s, rows, tile):
        out[s, rows, :] = b[s, rows, :] + known[s, rows, :] + tile

    products([faces.at[1]], [v], B, emit)


def fine_down_kernel(
    known, beside, faces, table, first,
    r0, right, f0, sent, longer, v1, v2, wide,
):
    index, inside = chosen(beside[128:136, :].astype(jnp.int32)[0:1], row(table, F_LINK + 2), 64, 128)
    expand(beside[0:128, :].reshape(S, 32, LANES), index, v2, inside)

    def emit_residual(s, rows, tile):
        r0[s, rows, :] = known[s, rows, :] + tile

    products([faces.at[2]], [v2], B, emit_residual)
    residual = r0[...]
    v1[...] = take_lanes(residual, row(table, F_PICK))
    v2[...] = take_lanes(residual, row(table, F_PICK + 1))
    wide[...] = take_lanes(residual, row(table, F_COARSE))
    right[...] = pack(wide[...], 2)

    def emit_right(s, rows, tile):
        right[s, rows, :] += tile

    products([first.at[F_WEIGHT], first.at[F_WEIGHT + 1]], [v1, v2], 32, emit_right)
    expand(right[...], lane_index() % 64, wide)
    mask = (row(table, M_POS) >= 32).astype(jnp.float32)

    def emit_field(s, rows, tile):
        f0[s, rows, :] = tile * mask

    products([first.at[M_INVERSE]], [wide], 32, emit_field)
    expand(f0[...], row(table, M_FINE), wide)
    sent[0:64, :] = pack(wide[...], 4).reshape(64, LANES)
    sent[64:72, :] = table[M_POS:F_POS, :].astype(jnp.float32)
    copy_out(sent, longer)


def middle_local_kernel(
    b, f0, table, m_diag, m_faces, c_inverse, m_weights, out, middle, coarse, own, linked
):
    pack_halves([m_diag, m_faces.at[0]], middle)
    pack_quarters([c_inverse, m_weights.at[0], m_weights.at[1]], coarse)
    expand(-f0[...], lane_index() % 64, own)
    expand(f0[...], row(table, M_LINK), linked)

    def emit(s, rows, tile):
        out[s, rows, :] = b[s, rows, :] + tile

    products([middle.at[M_DIAG], middle.at[M_FACE]], [own, linked], 32, emit)


def middle_flow_kernel(known, up, first, table, flow, out, v):
    index, inside = chosen(up[64:72, :].astype(jnp.int32)[0:1], row(table, M_LINK + 1), 32, 64)
    expand(up[0:64, :].reshape(S, 16, LANES), index, v, inside * gate_of(flow))

    def emit(s, rows, tile):
        out[s, rows, :] = known[s, rows, :] + tile

    products([first.at[M_NEXT]], [v], 32, emit)


def middle_down_kernel(
    known, beside, blocks, coarse, table, flow,
    r0, right, first, longer, v1, v2, wide,
):
    index, inside = chosen(beside[64:72, :].astype(jnp.int32)[0:1], row(table, M_LINK + 2), 32, 64)
    expand(beside[0:64, :].reshape(S, 16, LANES), index, v2, inside)

    def emit_residual(s, rows, tile):
        r0[s, rows, :] = known[s, rows, :] + tile

    products([blocks.at[M_NEXT + 1]], [v2], 32, emit_residual)
    residual = r0[...]
    expand(residual, row(table, M_PICK), v1)
    expand(residual, row(table, M_PICK + 1), v2)
    expand(residual, row(table, M_COARSE), wide)
    right[...] = pack(wide[...], 4)

    def emit_right(s, rows, tile):
        right[s, rows, :] += tile

    products([coarse.at[M_WEIGHT], coarse.at[M_WEIGHT + 1]], [v1, v2], 16, emit_right)
    expand(right[...], lane_index() % 32, wide)
    start = (flow[0] == 0).astype(jnp.float32)

    def emit_first(s, rows, tile):
        first[s, rows, :] = tile * start

    products([coarse.at[C_INVERSE]], [wide], 16, emit_first)
    copy_field(first, longer)


def coarse_first_kernel(right, own, c_faces, table, out, faces, wide):
    pack_quarters([c_faces.at[0], c_faces.at[1], c_faces.at[2]], faces)
    coarse_local_kernel(right, own, faces, table, out, wide)


def coarse_fine_kernel(right, own, faces, table, f_inverse, f_faces, out, chosen_fine, wide):
    select_fine([f_inverse, f_faces.at[1], f_faces.at[2]], table, chosen_fine)
    coarse_local_kernel(right, own, faces, table, out, wide)


def coarse_middle_kernel(right, own, faces, table, first, out, chosen_middle, wide):
    sources = [first.at[M_INVERSE], first.at[M_NEXT], first.at[M_NEXT + 1]]
    select_middle(sources, table, chosen_middle)
    coarse_local_kernel(right, own, faces, table, out, wide)


def coarse_local_kernel(right, own, faces, table, out, wide):
    expand(own[...], row(table, C_LINK), wide)

    def emit(s, rows, tile):
        out[s, rows, :] = right[s, rows, :] + tile

    products([faces.at[0]], [wide], 16, emit)


def coarse_flow_kernel(known, up, faces, table, flow, out, v):
    expand(up[...], row(table, C_LINK + 1), v, gate_of(flow))

    def emit(s, rows, tile):
        out[s, rows, :] = known[s, rows, :] + tile

    products([faces.at[1]], [v], 16, emit)


def coarse_step_kernel(step, known, own, beside, coarse, faces, table, flow, out, longer, v1, v2, total):
    gate = (step > flow[0]).astype(jnp.float32)
    expand(beside[0:64, :].reshape(S, 16, LANES), row(table, C_LINK + 2), v2, gate)

    def emit_total(s, rows, tile):
        total[s, rows, :] = known[s, rows, :] + tile

    products([faces.at[2]], [v2], 16, emit_total)
    expand(total[...], lane_index() % 32, v1)
    sweep = jnp.broadcast_to(step - flow[0], (8, LANES))

    def emit(s, rows, tile):
        fresh = jnp.where(sweep >= 0, tile, 0.0)
        out[s, rows, :] = jnp.where(sweep < SWEEPS, fresh, own[s, rows, :])

    products([coarse.at[C_INVERSE]], [v1], 16, emit)
    copy_field(out, longer)


def middle_up_local_kernel(r0, f0, fix, up, up_place, middle, chosen_middle, table, flow, out, base, own, linked, known):
    place = row(table, M_POS)
    index, inside = chosen(place, lane_index() % 64, 0, 32)
    expand(fix[...], index, own, inside)
    base[...] = f0[...] + pack(own[...], 2)
    own[...] = -own[...]
    index, inside = chosen(place, row(table, M_LINK), 0, 32)
    expand(fix[...], index, linked, inside)

    def emit(s, rows, tile):
        known[s, rows, :] = r0[s, rows, :] + tile

    products([middle.at[M_DIAG], middle.at[M_FACE]], [own, linked], 32, emit)
    expand(known[...], row(table, M_FINE), own)
    link = pick(row(table, M_LINK + 1), row(table, M_FINE))
    index, inside = chosen(up_place[64:72, :].astype(jnp.int32)[0:1], link, 0, 32)
    expand(up[...], index, linked, inside * gate_of(flow))
    out[...] = pack(own[...], 4)

    def emit_flow(s, rows, tile):
        out[s, rows, :] += tile

    products([chosen_middle.at[1]], [linked], 16, emit_flow)


def middle_up_kernel(known, base, beside, beside_place, chosen_middle, table, out, longer, v1, v2, total, result):
    link = pick(row(table, M_LINK + 2), row(table, M_FINE))
    index, inside = chosen(beside_place[64:72, :].astype(jnp.int32)[0:1], link, 0, 32)
    expand(beside[0:64, :].reshape(S, 16, LANES), index, v1, inside)

    def emit_total(s, rows, tile):
        total[s, rows, :] = known[s, rows, :] + tile

    products([chosen_middle.at[2]], [v1], 16, emit_total)
    expand(total[...], lane_index() % 32, v2)

    def emit(s, rows, tile):
        result[s, rows, :] = tile

    products([chosen_middle.at[0]], [v2], 16, emit)
    index, inside = chosen(row(table, M_POS), lane_index() % 64, 32, 64)
    expand(result[...], index, v1, inside)
    out[...] = base[...] + pack(v1[...], 2)
    copy_field(out, longer)


def fine_up_local_kernel(r0, f0, fix, diag, faces, table, out, base, own, linked, known):
    place = row(table, F_POS)
    index, inside = chosen(place, lane_index(), 0, 64)
    expand(fix[...], index, own, inside)
    base[...] = f0[...] + own[...]
    own[...] = -own[...]
    index, inside = chosen(place, row(table, F_LINK), 0, 64)
    expand(fix[...], index, linked, inside)

    def emit(s, rows, tile):
        known[s, rows, :] = r0[s, rows, :] + tile

    products([diag, faces.at[0]], [own, linked], B, emit)
    own[...] = take_lanes(known[...], row(table, F_FINE))
    out[...] = pack(own[...], 2)


def fine_up_flow_kernel(known, up, up_place, chosen_fine, table, flow, out, v):
    link = pick(row(table, F_LINK + 1), row(table, F_FINE))
    index, inside = chosen(up_place[128:136, :].astype(jnp.int32)[0:1], link, 0, 64)
    expand(up[...], index, v, inside * gate_of(flow))

    def emit(s, rows, tile):
        out[s, rows, :] = known[s, rows, :] + tile

    products([chosen_fine.at[1]], [v], 32, emit)


def fine_up_kernel(known, base, beside, beside_place, chosen_fine, table, out, v1, v2, total, result):
    link = pick(row(table, F_LINK + 2), row(table, F_FINE))
    index, inside = chosen(beside_place[128:136, :].astype(jnp.int32)[0:1], link, 0, 64)
    expand(beside[0:128, :].reshape(S, 32, LANES), index, v1, inside)

    def emit_total(s, rows, tile):
        total[s, rows, :] = known[s, rows, :] + tile

    products([chosen_fine.at[2]], [v1], 32, emit_total)
    expand(total[...], lane_index() % 64, v2)

    def emit(s, rows, tile):
        result[s, rows, :] = tile

    products([chosen_fine.at[0]], [v2], 32, emit)
    index, inside = chosen(row(table, F_POS), lane_index(), 64, 128)
    expand(result[...], index, v1, inside)
    out[...] = base[...] + v1[...]


WIDE = pltpu.VMEM((S, B, LANES), jnp.float32)


def f32(*shape):
    return jax.ShapeDtypeStruct(shape, jnp.float32)


def bf16(*shape):
    return jax.ShapeDtypeStruct(shape, jnp.bfloat16)


def call(kernel, operands, outs, scratch=(), work=1.0, flow=None, space=pltpu.VMEM, limit=40 * 1024, out_spaces=None):
    specs = [pl.BlockSpec(memory_space=space)] * len(operands)
    if flow is not None:
        specs.append(pl.BlockSpec(memory_space=pltpu.SMEM))
        operands = (*operands, flow)
    return pl.pallas_call(
        kernel,
        out_shape=outs,
        in_specs=specs,
        out_specs=jax.tree.map(lambda _: pl.BlockSpec(memory_space=pltpu.VMEM), outs)
        if out_spaces is None
        else tuple(pl.BlockSpec(memory_space=x) for x in out_spaces),
        scratch_shapes=list(scratch),
        compiler_params=pltpu.CompilerParams(vmem_limit_bytes=limit * 1024),
        cost_estimate=pl.CostEstimate(
            flops=int(work * 4_000_000), bytes_accessed=int(work * 1_000_000), transcendentals=0
        ),
    )(*operands)


def from_behind(block, axis):
    size = lax.axis_size(axis)
    return lax.ppermute(block, axis, [(i, (i + 1) % size) for i in range(size)])


def iterate_from_behind(block, step):
    flow_size, tiles = lax.axis_size("flow"), lax.axis_size("tile")
    route = []
    for g in range(flow_size):
        sends = 0 <= step - 1 - g < SWEEPS - 1
        for t in range(tiles):
            route.append((g * tiles + t, g * tiles + ((t + 1) % tiles if sends else t ^ 1)))
    return lax.ppermute(block, ("flow", "tile"), route)


def own_part(array):
    return array[0, 0]


def shards(*arrays):
    (
        b, f_diag, f_inverse, f_faces, f_links, f_order, f_picks, f_weights,
        m_diag, m_inverse, m_faces, m_links, m_order, m_picks, m_weights,
        c_inverse, c_faces, c_links,
    ) = map(own_part, arrays)
    flow_size = lax.axis_size("flow")
    flow = lax.axis_index("flow").astype(jnp.int32).reshape(1)
    f_order = f_order.reshape(1, LANES)
    m_order = m_order.reshape(1, 64)
    f_links, m_links, c_links = (x.reshape(3, 1, -1) for x in (f_links, m_links, c_links))
    c_inverse, c_faces, m_weights = (jnp.swapaxes(x, -1, -2) for x in (c_inverse, c_faces, m_weights))

    f0, f_linked, f_sent, f_longer, table = call(
        start_kernel,
        (b, f_inverse, f_links, f_order, f_picks, m_links, m_order, m_picks, c_links),
        (
            f32(S, B, LANES), f32(S, B, LANES), f32(136, LANES), f32(136 + SPARE, LANES),
            jax.ShapeDtypeStruct((TABLE, LANES), jnp.int32),
        ),
        (
            WIDE,
            pltpu.VMEM((B, B, LANES), jnp.bfloat16),
            *[pltpu.VMEM(x.shape, jnp.int32) for x in (f_links, f_order, f_picks, m_links, m_order, m_picks, c_links)],
            pltpu.SemaphoreType.DMA((9 + CHUNKS,)),
        ),
        space=pltpu.HBM,
        limit=65000,
    )
    f_beside, f_up = from_behind(f_longer, "tile"), from_behind(f_sent, "flow")
    known, first = call(
        fine_local_kernel,
        (f0, f_linked, f_diag, f_faces, m_inverse, f_weights, m_faces),
        (f32(S, B, LANES), bf16(5, 32, B, LANES)),
        (
            WIDE,
            WIDE,
            pltpu.VMEM((B, B, LANES), jnp.bfloat16),
            pltpu.VMEM((B, B, LANES), jnp.bfloat16),
            pltpu.VMEM(m_inverse.shape, jnp.bfloat16),
            pltpu.VMEM(f_weights.shape, jnp.bfloat16),
            pltpu.VMEM((2, B, B, 64), jnp.bfloat16),
            pltpu.VMEM((5, 32, B, LANES), jnp.bfloat16),
            pltpu.SemaphoreType.DMA((8,)),
            WIDE,
        ),
        3.0,
        space=pltpu.HBM,
        limit=55000,
        out_spaces=(pltpu.VMEM, pltpu.HBM),
    )
    known = call(fine_flow_kernel, (b, known, f_up, f_faces, table), f32(S, B, LANES), (WIDE,), 0.0, flow)
    f_r0, right, m_f0, m_sent, m_longer = call(
        fine_down_kernel,
        (known, f_beside, f_faces, table, first),
        (f32(S, B, LANES), f32(S, 32, LANES), f32(S, 32, LANES), f32(72, LANES), f32(72 + SPARE, LANES)),
        (WIDE, WIDE, WIDE),
        2.5,
    )
    m_beside, m_up = from_behind(m_longer, "tile"), from_behind(m_sent, "flow")
    known, middle, coarse = call(
        middle_local_kernel,
        (right, m_f0, table, m_diag, m_faces, c_inverse, m_weights),
        (f32(S, 32, LANES), bf16(2, 32, B, LANES), bf16(3, 16, B, LANES)),
        (WIDE, WIDE),
        2.0,
    )
    known = call(middle_flow_kernel, (known, m_up, first, table), f32(S, 32, LANES), (WIDE,), 0.0, flow)
    m_r0, right, value, longer = call(
        middle_down_kernel,
        (known, m_beside, first, coarse, table),
        (f32(S, 32, LANES), f32(S, 16, LANES), f32(S, 16, LANES), f32(64 + SPARE, LANES)),
        (WIDE, WIDE, WIDE),
        1.5,
        flow,
    )
    packed16 = pltpu.VMEM((S, 16, LANES), jnp.float32)
    packed32 = pltpu.VMEM((S, 32, LANES), jnp.float32)
    for step in range(1, SWEEPS + flow_size - 1):
        beside, up = iterate_from_behind(longer, step), from_behind(value, "flow")
        if step == 1:
            known, faces = call(
                coarse_first_kernel,
                (right, value, c_faces, table),
                (f32(S, 16, LANES), bf16(3, 16, B, LANES)),
                (WIDE,),
            )
        elif step == 2:
            known, chosen_fine = call(
                coarse_fine_kernel,
                (right, value, faces, table, f_inverse, f_faces),
                (f32(S, 16, LANES), bf16(3, 32, B, LANES)),
                (WIDE,),
            )
        elif step == 3:
            known, chosen_middle = call(
                coarse_middle_kernel,
                (right, value, faces, table, first),
                (f32(S, 16, LANES), bf16(3, 16, B, LANES)),
                (WIDE,),
            )
        else:
            known = call(coarse_local_kernel, (right, value, faces, table), f32(S, 16, LANES), (WIDE,), 0.25)
        known = call(coarse_flow_kernel, (known, up, faces, table), f32(S, 16, LANES), (WIDE,), 0.0, flow)
        value, longer = call(
            functools.partial(coarse_step_kernel, step),
            (known, value, beside, coarse, faces, table),
            (f32(S, 16, LANES), f32(64 + SPARE, LANES)),
            (WIDE, WIDE, packed16),
            0.5,
            flow,
        )
    beside = from_behind(longer, "tile")
    known, base = call(
        middle_up_local_kernel,
        (m_r0, m_f0, value, up, m_up, middle, chosen_middle, table),
        (f32(S, 16, LANES), f32(S, 32, LANES)),
        (WIDE, WIDE, packed32),
        1.25,
        flow,
    )
    fix, longer = call(
        middle_up_kernel,
        (known, base, beside, m_beside, chosen_middle, table),
        (f32(S, 32, LANES), f32(128 + SPARE, LANES)),
        (WIDE, WIDE, packed16, packed16),
        0.5,
    )
    beside, up = from_behind(longer, "tile"), from_behind(fix, "flow")
    known, base = call(
        fine_up_local_kernel,
        (f_r0, f0, fix, f_diag, f_faces, table),
        (f32(S, 32, LANES), f32(S, B, LANES)),
        (WIDE, WIDE, WIDE),
        2.0,
    )
    known = call(fine_up_flow_kernel, (known, up, f_up, chosen_fine, table), f32(S, 32, LANES), (WIDE,), 0.0, flow)
    field = call(
        fine_up_kernel,
        (known, base, beside, f_beside, chosen_fine, table),
        f32(S, B, LANES),
        (WIDE, WIDE, packed32, packed32),
        1.0,
    )
    return field[None, None]


def solution(mesh):
    ranks = (5, 5, 5, 6, 4, 3, 4, 6, 5, 5, 6, 4, 3, 4, 6, 5, 6, 4)
    return jax.shard_map(
        shards,
        mesh=mesh,
        in_specs=tuple(P("flow", "tile", *[None] * (rank - 2)) for rank in ranks),
        out_specs=P("flow", "tile", None, None, None),
        check_vma=False,
    )
```
